128 devices in a mesh: dp: 8 (over x, core), seq: 8 (over z_hi, y), tensor: 2 (over z_lo).
Axes of the slice: x: 4, y: 4, z: 4 (z_hi: 2, z_lo: 2; z = z_hi * 2 + z_lo), core: 2. Of those that a mesh axis runs over, the one named last changes fastest.
Arguments:
- hidden_in: bfloat16 [8, 1024, 2048], P('dp', 'seq'), may hold values from -6 to 6
- grad_out: bfloat16 [8, 1024, 2048], P('dp', 'seq'), may hold values from -6 to 6
- expert_ids: int32 [8, 1024, 4], P('dp', 'seq'), may hold values from 0 to 7, all different within a row
- slot_rank: int32 [8, 1024, 4], P('dp', 'seq'), may hold values from 0 to 511, as said below
- piece_start: int32 [8, 2], P('dp'), may hold values from 0 to 768, as said below
- norm_attn: bfloat16 [2048], P(('dp', 'seq')), may hold values from 0.5 to 1.5
- w_qkv: bfloat16 [2048, 3, 2048], P(('dp', 'seq'), None, 'tensor'), may hold values from -0.125 to 0.125
- b_qkv: bfloat16 [3, 16, 128], P(None, 'tensor', ('dp', 'seq')), may hold values from -1.796875 to 1.796875
- w_proj: bfloat16 [2048, 2048], P('tensor', ('dp', 'seq')), may hold values from -1 to 1
- norm_ffn: bfloat16 [2048], P(('dp', 'seq')), may hold values from 0.5 to 1.5
- w_router: bfloat16 [2048, 8], P(('dp', 'seq')), may hold values from -0.0625 to 0.0625
- w_share_gate: bfloat16 [2048], P(('dp', 'seq')), may hold values from -0.125 to 0.125
- expert_gate_up: bfloat16 [2048, 8, 2, 1408], P(('dp', 'seq'), None, None, 'tensor'), may hold values from -0.125 to 0.125
- expert_down: bfloat16 [8, 1408, 2048], P(None, 'tensor', ('dp', 'seq')), may hold values from -0.4375 to 0.4375
- shared_gate_up: bfloat16 [2048, 2, 5632], P(('dp', 'seq'), None, 'tensor'), may hold values from -0.125 to 0.125
- shared_down: bfloat16 [5632, 2048], P('tensor', ('dp', 'seq')), may hold values from -0.15625 to 0.15625
Outputs:
- hidden_out: bfloat16 [8, 1024, 2048], P('dp', 'seq')
- grad_in: float32 [8, 1024, 2048], P('dp', 'seq')
- grad_norm_attn: float32 [2048], P(('dp', 'seq'))
- grad_w_qkv: float32 [2048, 3, 2048], P(('dp', 'seq'), None, 'tensor')
- grad_b_qkv: float32 [3, 16, 128], P(None, 'tensor', ('dp', 'seq'))
- projection_weight_gradient: float32 [2048, 2048], P('tensor', ('dp', 'seq'))
- grad_norm_ffn: float32 [2048], P(('dp', 'seq'))
- grad_w_router: float32 [2048, 8], P(('dp', 'seq'))
- grad_share_gate: float32 [2048], P(('dp', 'seq'))
- grad_expert_gate_up: float32 [2048, 8, 2, 1408], P(('dp', 'seq'), None, None, 'tensor')
- expert_down_gradient: float32 [8, 1408, 2048], P(None, 'tensor', ('dp', 'seq'))
- grad_shared_gate_up: float32 [2048, 2, 5632], P(('dp', 'seq'), None, 'tensor')
- grad_shared_down: float32 [5632, 2048], P('tensor', ('dp', 'seq'))
The draws below stay inside these ranges and needn't reach their ends.
Inputs may be any that keep to these rules, and one draw needn't show every extreme that they name: `expert_ids`: each token names 4 different experts. `slot_rank`: in every aligned block of 128 tokens of a sequence, the 512 entries take each value once. `piece_start`: the 2 picture pieces of a sequence, 256 tokens each, lie in increasing order, apart from each other and inside the sequence.
All inputs are finite; a program needn't handle non-finite values.
Results may differ from the reference program's by a relative error of at most 0.025.
Values may be sent and summed in bfloat16 or wider, within the bound.
No kernel may reach another device: no remote copies, remote signals or barrier semaphores. Data moves between devices by JAX's collectives and lax.ppermute only.
A program may use at most 576 MiB of HBM per device.

```python
import math
import jax
import jax.numpy as jnp
from jax import lax

D = 2048
HEADS = 16
HD = 128
FE = 1408
FS = 5632
TOPK = 4
E = 8
PIC = 256
PIECES = 2
QW = 2048
SEQ_LEN = 1024
ROWS = 128
SEQS = 8
CAP = 80


def permute_block(block_key):
    return jax.random.permutation(block_key, ROWS * TOPK)


def draw_slot_rank(key, part):
    key = jax.random.fold_in(key, 11)
    blocks = SEQS * (SEQ_LEN // ROWS)
    block_keys = jax.random.split(key, blocks)
    orders = jax.vmap(permute_block)(block_keys)
    return orders.reshape(SEQS, SEQ_LEN, TOPK).astype(jnp.int32)


def draw_piece_start(key, part):
    key = jax.random.fold_in(key, 23)
    offset_key, pick_key = jax.random.split(key)
    room = SEQ_LEN // PIECES
    offsets = jax.random.randint(offset_key, (SEQS, PIECES), 0, room - PIC + 1)
    starts = offsets + room * jnp.arange(PIECES, dtype=jnp.int32)[None, :]
    chosen = jax.random.randint(pick_key, (), 0, SEQS)
    row_hit = jnp.arange(SEQS, dtype=jnp.int32)[:, None] == chosen
    column = jnp.arange(PIECES, dtype=jnp.int32)[None, :]
    starts = jnp.where(row_hit & (column == 0), 0, starts)
    starts = jnp.where(row_hit & (column == PIECES - 1), SEQ_LEN - PIC, starts)
    return starts.astype(jnp.int32)


def level_of(stream_key, shape, pieces, low, high):
    level = 1.0
    for dim, blocks in pieces:
        steps = jax.random.uniform(jax.random.fold_in(jax.random.fold_in(stream_key, 6), dim), (blocks,), jnp.float32, low / len(pieces), high / len(pieces))
        level = level * jnp.repeat(jnp.exp(steps), shape[dim] // blocks).reshape((-1,) + (1,) * (len(shape) - 1 - dim))
    return level


def distinct(own_key, rows, amount, top, lift):
    ranking = jax.random.permutation(jax.random.fold_in(own_key, 1), amount)
    favour = ranking
    for power in range(3):
        favour = favour * favour // amount
    favour = favour * lift // amount
    tickets = jax.random.randint(jax.random.fold_in(own_key, 2), (rows, amount), 0, 4096) + favour
    holders = jax.random.permutation(jax.random.fold_in(own_key, 3), rows)[jnp.arange(amount) % rows]
    tickets = jnp.where(jnp.arange(rows)[:, None] == holders[None, :], 1 << 14, tickets)
    priority = tickets * amount + jnp.arange(amount)
    return lax.top_k(priority.astype(jnp.int32), top)[1].astype(jnp.int32)


def normal_values(key, extent, deviation, limit, pieces=(), kind=jnp.bfloat16):
    array = jax.random.normal(key, extent, jnp.float32) * deviation
    if len(pieces) > 0:
        array = level_of(key, extent, pieces, -0.22, 0.18) * array
    return jnp.clip(array, min=-limit, max=limit).astype(kind)


def setup_inputs(seed: int = 0) -> dict:
    streams_of = jax.random.split(jax.random.key(seed), 17)
    hidden_in = normal_values(streams_of[0], (SEQS, SEQ_LEN, D), 1.0, 6.0, ((0, 8), (1, 8)))
    grad_out = normal_values(streams_of[1], (SEQS, SEQ_LEN, D), 1.0, 6.0, ((0, 8), (1, 8)))
    expert_ids = distinct(streams_of[2], SEQS * SEQ_LEN, E, TOPK, 4096).reshape((SEQS, SEQ_LEN, TOPK))
    slot_rank = draw_slot_rank(jax.random.fold_in(streams_of[16], 71), 0)
    piece_start = draw_piece_start(jax.random.fold_in(streams_of[16], 71), 0)
    norm_attn = jnp.clip(1.0 + 0.1 * jax.random.normal(streams_of[5], (D,), jnp.float32), 0.5, 1.5).astype(jnp.bfloat16)
    w_qkv = normal_values(streams_of[6], (D, 3, QW), D ** -0.5, 0.125, ((0, 64), (2, 2)))
    b_qkv = normal_values(streams_of[7], (3, HEADS, HD), 0.3, 1.796875, ((1, 2), (2, 64)))
    w_proj = normal_values(streams_of[8], (QW, D), (QW // 64) ** -0.5, 1.0, ((0, 2), (1, 64)))
    norm_ffn = jnp.clip(1.0 + 0.1 * jax.random.normal(streams_of[9], (D,), jnp.float32), 0.5, 1.5).astype(jnp.bfloat16)
    w_router = normal_values(streams_of[10], (D, E), (4 * D) ** -0.5, 0.0625, ((0, 64),))
    w_share_gate = normal_values(streams_of[11], (D,), D ** -0.5, 0.125, ((0, 64),))
    expert_gate_up = normal_values(streams_of[12], (D, E, 2, FE), D ** -0.5, 0.125, ((0, 64), (3, 2)))
    expert_down = normal_values(streams_of[13], (E, FE, D), (FE // 8) ** -0.5, 0.4375, ((1, 2), (2, 64)))
    shared_gate_up = normal_values(streams_of[14], (D, 2, FS), D ** -0.5, 0.125, ((0, 64), (2, 2)))
    shared_down = normal_values(streams_of[15], (FS, D), (FS // 4) ** -0.5, 0.15625, ((0, 2), (1, 64)))
    return dict(hidden_in=hidden_in, grad_out=grad_out, expert_ids=expert_ids, slot_rank=slot_rank, piece_start=piece_start, norm_attn=norm_attn, w_qkv=w_qkv, b_qkv=b_qkv, w_proj=w_proj, norm_ffn=norm_ffn, w_router=w_router, w_share_gate=w_share_gate, expert_gate_up=expert_gate_up, expert_down=expert_down, shared_gate_up=shared_gate_up, shared_down=shared_down)


@jax.custom_vjp
def low(v):
    return lax.optimization_barrier(v.astype(jnp.bfloat16)).astype(jnp.float32)

@jax.custom_vjp
def low_back(v):
    return v

def low_keep(v):
    return (low(v), None)

def low_pass(kept, grad):
    return (grad,)

def back_keep(v):
    return (v, None)

def back_low(kept, grad):
    return (low(grad),)
low.defvjp(low_keep, low_pass)
low_back.defvjp(back_keep, back_low)
EPS = 1e-06
THETA = 1000000.0
MASKED = -1000000000.0
HIGHEST = lax.Precision.HIGHEST

def rms_scale(values):
    return lax.rsqrt(lax.optimization_barrier(jnp.mean(values * values, axis=-1, keepdims=True)) + EPS)

def rotary_angle_tables(positions):
    half_dim = HD // 2
    freq_table = jnp.exp(jnp.arange(half_dim, dtype=jnp.float32) * (-2.0 * math.log(THETA) / HD))
    angle = positions.astype(jnp.float32)[:, None] * freq_table[None, :]
    return (jnp.cos(angle), jnp.sin(angle))

def rotate(values, cosine_table, sine_table):
    half_dim = values.shape[-1] // 2
    lead_part = values[..., :half_dim]
    tail_part = values[..., half_dim:]
    cosine_h = cosine_table[:, None, :]
    sine_h = sine_table[:, None, :]
    return jnp.concatenate([lead_part * cosine_h - tail_part * sine_h, tail_part * cosine_h + lead_part * sine_h], axis=-1)

def piece_labels(positions, starts):
    inside = (positions[:, None] >= starts[None, :]) & (positions[:, None] < starts[None, :] + PIC)
    labels = jnp.arange(starts.shape[0], dtype=jnp.int32)
    return lax.optimization_barrier(jnp.max(jnp.where(inside, labels[None, :], -1), axis=1))

def visible(query_pos, key_pos, query_seg, key_seg):
    causal = key_pos[None, :] <= query_pos[:, None]
    picture = (query_seg[:, None] == key_seg[None, :]) & (query_seg[:, None] >= 0)
    return causal | picture

def slot_tables(ids_block, rank_block):
    flat_ids = ids_block.reshape(-1)
    flat_rank = rank_block.reshape(-1)
    earlier = (flat_rank[None, :] < flat_rank[:, None]) & (flat_ids[None, :] == flat_ids[:, None])
    position = lax.optimization_barrier(jnp.sum(earlier.astype(jnp.int32), axis=1))
    select_expert_index = (flat_ids[:, None] == jnp.arange(E, dtype=jnp.int32)[None, :]).astype(jnp.float32)
    pick_slot = (position[:, None] == jnp.arange(CAP, dtype=jnp.int32)[None, :]).astype(jnp.float32)
    return (select_expert_index.reshape(ROWS, TOPK, E), pick_slot.reshape(ROWS, TOPK, CAP))

def one_sequence(params, x_seq, ids_seq, rank_seq, start_seq):
    norm_attn, w_qkv, b_qkv, w_proj, norm_ffn, w_router, w_share_gate, expert_gate_up, expert_down, shared_gate_up, shared_down = params
    positions = jnp.arange(SEQ_LEN, dtype=jnp.int32)
    cosine_table, sine_table = rotary_angle_tables(positions)
    labels = piece_labels(positions, start_seq)
    allowed = visible(positions, positions, labels, labels)
    normed_one = low(x_seq * rms_scale(x_seq) * norm_attn)
    linear = jnp.einsum('ld,dtc->tlc', normed_one, w_qkv, precision=HIGHEST) + b_qkv.reshape(3, 1, QW)
    linear = low_back(linear)
    query_rot = low(rotate(linear[0].reshape(SEQ_LEN, HEADS, HD), cosine_table, sine_table))
    key_rot = low(rotate(linear[1].reshape(SEQ_LEN, HEADS, HD), cosine_table, sine_table))
    value_seq = low(linear[2].reshape(SEQ_LEN, HEADS, HD))
    scores = low_back(jnp.einsum('qhd,khd->hqk', query_rot, key_rot, precision=HIGHEST) * (1.0 / math.sqrt(HD)))
    scores = jnp.where(allowed[None], scores, MASKED)
    attn_probs = jax.nn.softmax(scores, axis=-1)
    attn_heads = low(low_back(jnp.einsum('hqk,khd->qhd', low(attn_probs), value_seq, precision=HIGHEST)))
    attn_total = low_back(jnp.dot(attn_heads.reshape(SEQ_LEN, QW), w_proj, precision=HIGHEST))
    after_attn = x_seq + attn_total
    ffn_normalized_input = low(after_attn * rms_scale(after_attn) * norm_ffn)
    logits = low_back(jnp.dot(ffn_normalized_input, w_router, precision=HIGHEST))
    router_probs = jax.nn.softmax(logits, axis=-1)
    share_sig = jax.nn.sigmoid(low_back(jnp.dot(ffn_normalized_input, w_share_gate, precision=HIGHEST)))
    blocks = SEQ_LEN // ROWS
    select_expert_index, pick_slot = jax.vmap(slot_tables)(ids_seq.reshape(blocks, ROWS, TOPK), rank_seq.reshape(blocks, ROWS, TOPK))
    probs_block = router_probs.reshape(blocks, ROWS, E)
    gate_vals = lax.optimization_barrier(jnp.sum(probs_block[:, :, None, :] * select_expert_index, axis=-1))
    dispatch = jnp.einsum('nrke,nrkc->necr', select_expert_index, pick_slot)
    combine = jnp.einsum('nrke,nrkc,nrk->nrec', select_expert_index, pick_slot, gate_vals, precision=HIGHEST)
    expert_in = jnp.einsum('necr,nrd->necd', dispatch, ffn_normalized_input.reshape(blocks, ROWS, D), precision=HIGHEST)
    gate_up_product = low_back(jnp.einsum('necd,detf->netcf', expert_in, expert_gate_up, precision=HIGHEST))
    expert_act = low(jax.nn.silu(gate_up_product[:, :, 0]) * gate_up_product[:, :, 1])
    expert_out = low_back(jnp.einsum('necf,efd->necd', expert_act, expert_down, precision=HIGHEST))
    routed = jnp.einsum('nrec,necd->nrd', combine, expert_out, precision=HIGHEST).reshape(SEQ_LEN, D)
    shared_hidden_activation = low_back(jnp.einsum('ld,dtf->tlf', ffn_normalized_input, shared_gate_up, precision=HIGHEST))
    shared_act = low(jax.nn.silu(shared_hidden_activation[0]) * shared_hidden_activation[1])
    shared_expert_output = low_back(jnp.dot(shared_act, shared_down, precision=HIGHEST))
    return after_attn + routed + share_sig[:, None] * shared_expert_output

def reference(hidden_in, grad_out, expert_ids, slot_rank, piece_start, norm_attn, w_qkv, b_qkv, w_proj, norm_ffn, w_router, w_share_gate, expert_gate_up, expert_down, shared_gate_up, shared_down):
    params = tuple((weight.astype(jnp.float32) for weight in (norm_attn, w_qkv, b_qkv, w_proj, norm_ffn, w_router, w_share_gate, expert_gate_up, expert_down, shared_gate_up, shared_down)))

    def forward(inputs, weights):

        def scan_step(carry_in, seq_item):
            x_seq, ids_seq, rank_seq, start_seq = seq_item
            return (carry_in, jax.checkpoint(one_sequence)(weights, x_seq, ids_seq, rank_seq, start_seq))
        carry_end, outputs = lax.scan(scan_step, jnp.zeros((), jnp.float32), (inputs, expert_ids, slot_rank, piece_start))
        return outputs
    outputs, pullback = jax.vjp(forward, hidden_in.astype(jnp.float32), params)
    layer_input_gradient, weight_grads = pullback(grad_out.astype(jnp.float32))
    return (outputs.astype(jnp.bfloat16), layer_input_gradient, weight_grads[0], weight_grads[1], weight_grads[2], weight_grads[3], weight_grads[4], weight_grads[5], weight_grads[6], weight_grads[7], weight_grads[8], weight_grads[9], weight_grads[10])
```

```python
import math

import jax
import jax.numpy as jnp
from jax import lax
from jax.sharding import PartitionSpec as P

HD = 128
TOPK = 4
PIC = 256

EPS = 1e-06
THETA = 1000000.0
MASKED = -1000000000.0

GRID = ("seq", "tensor")
BF = jnp.bfloat16
F32 = jnp.float32
LANES = 128


def up_to(size, multiple):
    return -(-size // multiple) * multiple


def dot(a, b, dims):
    return lax.dot_general(a, b, (dims, ((), ())), preferred_element_type=F32)


def mm(a, b):
    return dot(a, b, ((1,), (0,)))


def mm_nt(a, b):
    return dot(a, b, ((1,), (1,)))


def mm_tn(a, b):
    return dot(a, b, ((0,), (0,)))


def rms_scale(values):
    return lax.rsqrt(jnp.mean(values * values, axis=-1, keepdims=True) + EPS)


def silu_grads(act_grad, gate_val, up_val):
    gate_sigmoid = jax.nn.sigmoid(gate_val)
    gate_grad = act_grad * up_val * gate_sigmoid * (1.0 + gate_val * (1.0 - gate_sigmoid))
    up_grad = act_grad * (gate_val * gate_sigmoid)
    return (gate_grad, up_grad)


def hop(x, mask):
    count = lax.axis_size("seq") * lax.axis_size("tensor")
    return lax.ppermute(x, GRID, [(i, i ^ mask) for i in range(count)])


Y_RING = (2, 6)
Z_RING = (1, 9)


def ring_gather(x, ring):
    one, three = ring
    half = x.shape[0] // 2
    from_one = hop(x, one)
    from_three = hop(x, three)
    low = hop(from_three[:half], one)
    high = hop(from_one[half:], three)
    return [x, from_one, jnp.concatenate([low, high], 0), from_three]


def ring_scatter(parts, ring):
    one, three = ring
    half = parts[0].shape[0] // 2
    far = parts[2].astype(BF)
    from_one = hop(far[half:], one).astype(F32)
    from_three = hop(far[:half], three).astype(F32)
    to_one = jnp.concatenate([parts[1][:half] + from_three, parts[1][half:]], 0)
    to_three = jnp.concatenate([parts[3][:half], parts[3][half:] + from_one], 0)
    return (
        parts[0]
        + hop(to_one.astype(BF), one).astype(F32)
        + hop(to_three.astype(BF), three).astype(F32)
    )


def plane_gather(x):
    n, width = x.shape
    half = n // 2
    y_first = jnp.concatenate(ring_gather(x[:half], Y_RING), 0)
    z_first = jnp.concatenate(ring_gather(x[half:], Z_RING), 0)
    y_first = jnp.stack(ring_gather(y_first, Z_RING)).reshape(4, 4, half, width)
    z_first = jnp.stack(ring_gather(z_first, Y_RING)).reshape(4, 4, half, width)
    pieces = []
    for high in range(2):
        for row in range(4):
            for low in range(2):
                z_at = 2 * high + low
                pieces.append(y_first[z_at, row])
                pieces.append(z_first[row, z_at])
    return jnp.concatenate(pieces, 0)


def plane_scatter(parts):
    rows, width = parts.shape
    n = rows // 16
    half = n // 2
    parts = parts.reshape(2, 4, 2, n, width)
    z_first = [
        parts[high, :, low, :half].reshape(4 * half, width) for high in (0, 1) for low in (0, 1)
    ]
    y_first = [parts[:, row, :, half:].reshape(4 * half, width) for row in range(4)]
    z_sum = ring_scatter(z_first, Z_RING).reshape(4, half, width)
    y_sum = ring_scatter(y_first, Y_RING).reshape(4, half, width)
    a = ring_scatter([z_sum[i] for i in range(4)], Y_RING)
    b = ring_scatter([y_sum[i] for i in range(4)], Z_RING)
    return jnp.concatenate([a, b], 0)


def flip_blocks(x, index):
    for bit in (1, 2, 4):
        order = [p ^ bit for p in range(8)]
        swapped = jnp.concatenate([x[p : p + 1] for p in order], 0)
        x = jnp.where((index & bit) != 0, swapped, x)
    return x


def body(
    hidden_in,
    grad_out,
    expert_ids,
    slot_rank,
    piece_start,
    norm_attn,
    w_qkv,
    b_qkv,
    w_proj,
    norm_ffn,
    w_router,
    w_share_gate,
    expert_gate_up,
    expert_down,
    shared_gate_up,
    shared_down,
):
    seqs = lax.axis_size("seq")
    dps = lax.axis_size("dp")
    me_seq = lax.axis_index("seq")
    me_tensor = lax.axis_index("tensor")
    me = me_seq * 2 + me_tensor
    rows = hidden_in.shape[1]
    own = rows // 2
    length = rows * seqs
    depth = w_qkv.shape[0]
    width = depth * dps * seqs
    experts = expert_gate_up.shape[1]
    fe = expert_gate_up.shape[3]
    fs = shared_gate_up.shape[2] // seqs
    fe_pad = up_to(fe, LANES)
    fs_pad = up_to(fs, LANES)
    bias_part = b_qkv.shape[2]
    heads = b_qkv.shape[1]
    capacity = (5 * rows * TOPK + 4 * experts - 1) // (4 * experts)
    score_scale = 1.0 / math.sqrt(HD)

    def mine(x):
        return lax.dynamic_slice_in_dim(x, me_tensor * own, own, 0)

    def both_halves(x):
        other = hop(x, 1)
        first = jnp.where(me_tensor == 0, x, other)
        second = jnp.where(me_tensor == 0, other, x)
        return jnp.concatenate([first, second], 0)

    x_own = mine(hidden_in[0])
    x_all = plane_gather(x_own)

    misc = jnp.concatenate(
        [norm_attn[:, None], norm_ffn[:, None], w_share_gate[:, None], w_router], axis=1
    )
    n_misc = misc.shape[1]
    bias_rows = b_qkv.transpose(1, 0, 2).reshape(heads, 3 * bias_part)
    bias_rows = jnp.pad(bias_rows, ((0, 0), (0, depth - 3 * bias_part)))
    attn_blob = jnp.concatenate(
        [
            w_qkv.reshape(depth, 3, heads, HD).transpose(2, 0, 1, 3).reshape(heads, depth, 3 * HD),
            jnp.broadcast_to(misc[None], (heads, depth, n_misc)),
            bias_rows[:, :, None],
            jnp.zeros((heads, depth, LANES - n_misc - 1), BF),
        ],
        axis=2,
    )
    attn_blob = lax.all_to_all(attn_blob, "seq", 0, 0, tiled=True)
    attn_full = lax.all_gather(
        attn_blob.reshape(seqs * depth, 3 * HD + LANES), "dp", axis=0, tiled=True
    )
    proj_full = lax.all_gather(w_proj.T, ("dp", "seq"), axis=0, tiled=True)
    qkv_full = attn_full[:, : 3 * HD]
    misc_full = attn_full[:, 3 * HD :]
    bias_full = misc_full[:, n_misc].reshape(dps * seqs, depth)[:, : 3 * bias_part]
    bias_full = bias_full.reshape(dps * seqs, 3, bias_part).transpose(1, 0, 2).reshape(1, 3 * HD)
    misc_rows = misc_full[:, :n_misc].T.astype(F32)
    gain_attn = misc_rows[0:1]
    gain_ffn = misc_rows[1:2]

    pad_e = ((0, 0), (0, 0), (0, 0), (0, fe_pad - fe))
    pad_s = ((0, 0), (0, 0), (0, 0), (0, fs_pad - fs))
    egu_blob = jnp.pad(expert_gate_up.transpose(1, 0, 2, 3), pad_e)
    edn_blob = jnp.pad(expert_down.transpose(0, 2, 1)[:, :, None], pad_e)
    sgu_blob = jnp.pad(
        shared_gate_up.reshape(depth, 2, seqs, fs).transpose(2, 0, 1, 3), pad_s
    )
    sdn_blob = jnp.pad(shared_down.reshape(seqs, fs, depth).transpose(0, 2, 1)[:, :, None], pad_s)
    ffn_blob = jnp.concatenate(
        [
            egu_blob.reshape(seqs, depth, 2 * fe_pad),
            edn_blob.reshape(seqs, depth, fe_pad),
            sgu_blob.reshape(seqs, depth, 2 * fs_pad),
            sdn_blob.reshape(seqs, depth, fs_pad),
        ],
        axis=2,
    )
    ffn_blob = lax.all_to_all(ffn_blob, "seq", 0, 0, tiled=True)
    ffn_full = lax.all_gather(
        ffn_blob.reshape(seqs * depth, 3 * fe_pad + 3 * fs_pad), "dp", axis=0, tiled=True
    )
    cut = [2 * fe_pad, 3 * fe_pad, 3 * fe_pad + 2 * fs_pad]
    egu = ffn_full[:, : cut[0]]
    edn = ffn_full[:, cut[0] : cut[1]]
    sgu = ffn_full[:, cut[1] : cut[2]]
    sdn = ffn_full[:, cut[2] :]

    flat_ids = expert_ids[0].reshape(-1)
    flat_rank = slot_rank[0].reshape(-1)
    earlier = (flat_rank[None, :] < flat_rank[:, None]) & (flat_ids[None, :] == flat_ids[:, None])
    position = jnp.sum(earlier.astype(jnp.int32), axis=1)
    position = jnp.where(position < capacity, position, LANES - 1)
    chosen = expert_ids[0][:, :, None] == jnp.arange(experts, dtype=jnp.int32)[None, None, :]
    slot_of = jnp.sum(
        jnp.where(chosen, position.reshape(rows, TOPK)[:, :, None] - (LANES - 1), 0), axis=1
    ) + (LANES - 1)
    slot_cols = jnp.pad(mine(slot_of).astype(BF), ((0, 0), (0, LANES - experts)))
    dy_own = mine(grad_out[0])
    dy_slots = plane_gather(jnp.concatenate([dy_own, slot_cols], 1))
    dy_all = dy_slots[:, :width]
    slots_all = dy_slots[:, width : width + experts].astype(jnp.int32)

    chunk = jnp.arange(2 * seqs, dtype=jnp.int32) ^ me
    positions = (chunk[:, None] * own + jnp.arange(own, dtype=jnp.int32)[None, :]).reshape(-1)
    freq_table = jnp.exp(jnp.arange(HD // 2, dtype=F32) * (-2.0 * math.log(THETA) / HD))
    angle = positions.astype(F32)[:, None] * freq_table[None, :]
    cosine = jnp.cos(angle)
    sine = jnp.sin(angle)
    starts = piece_start[0]
    inside = (positions[:, None] >= starts[None, :]) & (
        positions[:, None] < starts[None, :] + PIC
    )
    labels = jnp.arange(starts.shape[0], dtype=jnp.int32)
    segment = jnp.max(jnp.where(inside, labels[None, :], -1), axis=1)

    def seen():
        causal = positions[None, :] <= positions[:, None]
        picture = (segment[:, None] == segment[None, :]) & (segment[:, None] >= 0)
        return causal | picture

    def rotate(values):
        lead, tail = values[:, : HD // 2], values[:, HD // 2 :]
        return jnp.concatenate([lead * cosine - tail * sine, tail * cosine + lead * sine], axis=1)

    def unrotate(values):
        lead, tail = values[:, : HD // 2], values[:, HD // 2 :]
        return jnp.concatenate([lead * cosine + tail * sine, tail * cosine - lead * sine], axis=1)

    resid_all = x_all.astype(F32)
    norm_one = resid_all * rms_scale(resid_all)
    normed_one = (norm_one * gain_attn).astype(BF)
    linear = mm(normed_one, qkv_full) + bias_full.astype(F32)
    query = rotate(linear[:, :HD]).astype(BF)
    key = rotate(linear[:, HD : 2 * HD]).astype(BF)
    value = linear[:, 2 * HD :].astype(BF)
    scores = jnp.where(seen(), mm_nt(query, key) * score_scale, MASKED)
    exp_scores = jnp.exp(scores - jnp.max(scores, axis=1, keepdims=True))
    attn_probs = exp_scores / jnp.sum(exp_scores, axis=1, keepdims=True)
    probs_low = attn_probs.astype(BF)
    attn_head = mm(probs_low, value).astype(BF)

    by_block = flip_blocks(attn_head.reshape(seqs, rows, HD), me_seq)
    by_head = lax.all_to_all(by_block, "seq", 0, 0, tiled=True)
    attn_flat = by_head.transpose(1, 0, 2).reshape(rows, heads * HD)
    attn_part = mm_nt(attn_flat, proj_full)
    attn_sum = attn_part[:own] + hop(attn_part[own:].astype(BF), 1).astype(F32)
    after_attn = x_own.astype(F32) + attn_sum
    scale_two = rms_scale(after_attn)
    norm_two = after_attn * scale_two
    normed_two = (norm_two * gain_ffn).astype(BF)
    h_all = plane_gather(normed_two)

    logits_all = mm(h_all, misc_full)
    router_probs = jax.nn.softmax(logits_all[:, 3 : 3 + experts], axis=-1)
    share_sig = jax.nn.sigmoid(logits_all[:, 2:3])
    mine_e = jnp.arange(experts, dtype=jnp.int32)[None, :] == me_seq
    gate_all = jnp.sum(jnp.where(mine_e, router_probs, 0.0), axis=1)
    slot_all = jnp.sum(jnp.where(mine_e, slots_all, 0), axis=1)
    dispatch = (
        slot_all.reshape(seqs, 1, rows) == jnp.arange(capacity, dtype=jnp.int32)[None, :, None]
    )
    slot_gate = jnp.sum(
        jnp.where(dispatch, gate_all.reshape(seqs, 1, rows), 0.0), axis=2
    ).reshape(seqs * capacity, 1)
    dispatch = dispatch.astype(BF)

    def to_slots(x):
        out = lax.dot_general(
            dispatch,
            x.reshape(seqs, rows, -1),
            (((2,), (1,)), ((0,), (0,))),
            preferred_element_type=F32,
        )
        return out.reshape(seqs * capacity, -1)

    def to_tokens(x):
        out = lax.dot_general(
            dispatch,
            x.reshape(seqs, capacity, -1),
            (((1,), (1,)), ((0,), (0,))),
            preferred_element_type=F32,
        )
        return out.reshape(length, -1)

    expert_in = to_slots(h_all).astype(BF)
    slot_dy = to_slots(dy_all)
    slot_dgate = (slot_gate * slot_dy).astype(BF)
    expert_gu = mm(expert_in, egu)
    expert_g, expert_u = expert_gu[:, :fe_pad], expert_gu[:, fe_pad:]
    expert_act = (jax.nn.silu(expert_g) * expert_u).astype(BF)
    expert_out = mm_nt(expert_act, edn)
    slot_dot = jnp.sum(slot_dy * expert_out, axis=1)
    routed_part = to_tokens((slot_gate * expert_out).astype(BF))

    shared_gu = mm(h_all, sgu)
    shared_g, shared_u = shared_gu[:, :fs_pad], shared_gu[:, fs_pad:]
    shared_act = (jax.nn.silu(shared_g) * shared_u).astype(BF)
    shared_out = mm_nt(shared_act, sdn)
    upstream = dy_all.astype(F32)
    share_dot = jnp.sum(upstream * shared_out, axis=1)
    ffn_sum = plane_scatter(routed_part + share_sig * shared_out)
    hidden_out = both_halves((after_attn + ffn_sum).astype(BF))

    grad_edn = mm_tn(slot_dgate, expert_act)
    expert_da = mm(slot_dgate, edn)
    expert_dg, expert_du = silu_grads(expert_da, expert_g, expert_u)
    expert_dgu = jnp.concatenate([expert_dg.astype(BF), expert_du.astype(BF)], 1)
    grad_egu = mm_tn(expert_in, expert_dgu)
    expert_dx = mm_nt(expert_dgu, egu)
    shared_dy = (share_sig * upstream).astype(BF)
    grad_sdn = mm_tn(shared_dy, shared_act)
    shared_da = mm(shared_dy, sdn)
    shared_dg, shared_du = silu_grads(shared_da, shared_g, shared_u)
    shared_dgu = jnp.concatenate([shared_dg.astype(BF), shared_du.astype(BF)], 1)
    grad_sgu = mm_tn(h_all, shared_dgu)
    shared_dx = mm_nt(shared_dgu, sgu)
    route_dot = jnp.sum(
        dispatch.astype(F32) * slot_dot.reshape(seqs, capacity, 1), axis=1
    ).reshape(length, 1)
    dots = jnp.concatenate(
        [jnp.where(mine_e, route_dot, 0.0), share_dot[:, None]], 1
    )
    dots = jnp.pad(dots, ((0, 0), (0, LANES - experts - 1)))
    back = plane_scatter(
        jnp.concatenate([to_tokens(expert_dx.astype(BF)) + shared_dx, dots], 1)
    )

    ffn_grad = jnp.concatenate([grad_egu, grad_edn, grad_sgu, grad_sdn], 1).astype(BF)
    ffn_grad = lax.psum_scatter(ffn_grad, "dp", scatter_dimension=0, tiled=True)
    ffn_grad = lax.all_to_all(ffn_grad.reshape(seqs, depth, -1), "seq", 0, 0, tiled=True)
    ffn_grad = ffn_grad.astype(F32)
    out_egu = ffn_grad[:, :, : cut[0]].reshape(seqs, depth, 2, fe_pad)[..., :fe]
    out_egu = out_egu.transpose(1, 0, 2, 3)
    out_edn = ffn_grad[:, :, cut[0] : cut[0] + fe].transpose(0, 2, 1)
    out_sgu = ffn_grad[:, :, cut[1] : cut[2]].reshape(seqs, depth, 2, fs_pad)[..., :fs]
    out_sgu = out_sgu.transpose(1, 2, 0, 3).reshape(depth, 2, seqs * fs)
    out_sdn = ffn_grad[:, :, cut[2] : cut[2] + fs].transpose(0, 2, 1).reshape(seqs * fs, depth)

    probs_own = router_probs[:own]
    sig_own = share_sig[:own]
    dprobs = back[:, width : width + experts]
    dlogits = probs_own * (dprobs - jnp.sum(probs_own * dprobs, axis=1, keepdims=True))
    dshare = back[:, width + experts : width + experts + 1] * sig_own * (1.0 - sig_own)
    dmisc = jnp.concatenate([jnp.zeros((own, 2), F32), dshare, dlogits], 1)
    dmisc = jnp.pad(dmisc, ((0, 0), (0, LANES - n_misc))).astype(BF)
    dh_two = back[:, :width] + mm_nt(dmisc, misc_full)
    grad_misc = mm_tn(normed_two, dmisc)
    grad_gain_ffn = jnp.sum(dh_two * norm_two, axis=0)
    inner_two = dh_two * gain_ffn
    dx_one = dy_own.astype(F32) + scale_two * (
        inner_two - norm_two * jnp.mean(inner_two * norm_two, axis=-1, keepdims=True)
    )
    dx_low = dx_one.astype(BF)

    dx_pair = jnp.concatenate([dx_low, hop(dx_low, 1)], 0)
    do_flat = mm(dx_pair, proj_full).astype(BF)
    do_heads = do_flat.reshape(rows, heads, HD).transpose(1, 0, 2)
    do_blocks = lax.all_to_all(do_heads, "seq", 0, 0, tiled=True)
    do_head = flip_blocks(do_blocks, me_seq).reshape(length, HD)
    dx_all = plane_gather(dx_low)
    grad_proj = mm_tn(dx_all, attn_head)
    dvalue = mm_tn(probs_low, do_head)
    dprob = mm_nt(do_head, value)
    row_delta = jnp.sum(attn_probs * dprob, axis=1, keepdims=True)
    dscore = (attn_probs * (dprob - row_delta)).astype(BF)
    dquery = mm(dscore, key) * score_scale
    dkey = mm_tn(dscore, query) * score_scale
    dlinear = jnp.concatenate([unrotate(dquery), unrotate(dkey), dvalue], 1).astype(BF)
    grad_bias = jnp.sum(dlinear.astype(F32), axis=0)
    grad_qkv = mm_tn(normed_one, dlinear)
    dh_part = mm_nt(dlinear, qkv_full)
    grad_gain_attn = jnp.sum(dh_part * norm_one, axis=0)
    dh_one = plane_scatter(dh_part)
    resid = x_own.astype(F32)
    scale_one = rms_scale(resid)
    norm_own = resid * scale_one
    inner_one = dh_one * gain_attn
    grad_in = dx_one + scale_one * (
        inner_one - norm_own * jnp.mean(inner_one * norm_own, axis=-1, keepdims=True)
    )
    grad_in = both_halves(grad_in)

    bias_rows = grad_bias.reshape(3, dps * seqs, bias_part).transpose(1, 0, 2)
    bias_rows = bias_rows.reshape(dps * seqs, 3 * bias_part)
    bias_rows = jnp.pad(bias_rows, ((0, 0), (0, depth - 3 * bias_part))).reshape(width, 1)
    attn_grad = jnp.concatenate(
        [
            grad_qkv,
            grad_gain_attn[:, None],
            grad_gain_ffn[:, None],
            grad_misc[:, 2:n_misc],
            bias_rows,
            jnp.zeros((width, LANES - n_misc - 1), F32),
            grad_proj,
        ],
        1,
    ).astype(BF)
    attn_grad = lax.psum_scatter(attn_grad, "dp", scatter_dimension=0, tiled=True)
    attn_grad = lax.all_to_all(attn_grad.reshape(seqs, depth, -1), "seq", 0, 0, tiled=True)
    attn_grad = attn_grad.astype(F32)
    out_qkv = attn_grad[:, :, : 3 * HD].reshape(heads, depth, 3, HD)
    out_qkv = out_qkv.transpose(1, 2, 0, 3).reshape(depth, 3, heads * HD)
    out_misc = jnp.sum(attn_grad[:, :, 3 * HD : 3 * HD + n_misc], axis=0)
    out_misc = out_misc + hop(out_misc, 1)
    out_bias = attn_grad[:, : 3 * bias_part, 3 * HD + n_misc]
    out_bias = out_bias.reshape(heads, 3, bias_part).transpose(1, 0, 2)
    out_proj = attn_grad[:, :, 3 * HD + LANES :].transpose(0, 2, 1).reshape(heads * HD, depth)

    return (
        hidden_out[None],
        grad_in[None],
        out_misc[:, 0],
        out_qkv,
        out_bias,
        out_proj,
        out_misc[:, 1],
        out_misc[:, 3:n_misc],
        out_misc[:, 2],
        out_egu,
        out_edn,
        out_sgu,
        out_sdn,
    )


def solution(mesh):
    in_specs = (
        P("dp", "seq", None),
        P("dp", "seq", None),
        P("dp", "seq", None),
        P("dp", "seq", None),
        P("dp", None),
        P(("dp", "seq")),
        P(("dp", "seq"), None, "tensor"),
        P(None, "tensor", ("dp", "seq")),
        P("tensor", ("dp", "seq")),
        P(("dp", "seq")),
        P(("dp", "seq"), None),
        P(("dp", "seq")),
        P(("dp", "seq"), None, None, "tensor"),
        P(None, "tensor", ("dp", "seq")),
        P(("dp", "seq"), None, "tensor"),
        P("tensor", ("dp", "seq")),
    )
    out_specs = (
        P("dp", "seq", None),
        P("dp", "seq", None),
        P(("dp", "seq")),
        P(("dp", "seq"), None, "tensor"),
        P(None, "tensor", ("dp", "seq")),
        P("tensor", ("dp", "seq")),
        P(("dp", "seq")),
        P(("dp", "seq"), None),
        P(("dp", "seq")),
        P(("dp", "seq"), None, None, "tensor"),
        P(None, "tensor", ("dp", "seq")),
        P(("dp", "seq"), None, "tensor"),
        P("tensor", ("dp", "seq")),
    )
    return jax.shard_map(body, mesh=mesh, in_specs=in_specs, out_specs=out_specs, check_vma=False)
```

```python
import math

import jax
import jax.numpy as jnp
from jax import lax
from jax.experimental import pallas as pl
from jax.experimental.pallas import tpu as pltpu
from jax.sharding import Mesh
from jax.sharding import PartitionSpec as P

HD = 128
TOPK = 4
PIC = 256

EPS = 1e-06
THETA = 1000000.0
MASKED = -1000000000.0

SEQ = ("z_hi", "ring")
GRID = ("z_hi", "ring", "tensor")
BF = jnp.bfloat16
F32 = jnp.float32
LANES = 128


def up_to(size, multiple):
    return -(-size // multiple) * multiple


def dot(a, b, dims):
    return lax.dot_general(a, b, (dims, ((), ())), preferred_element_type=F32)


def mm(a, b):
    return dot(a, b, ((1,), (0,)))


def mm_nt(a, b):
    return dot(a, b, ((1,), (1,)))


def mm_tn(a, b):
    return dot(a, b, ((0,), (0,)))


def rms_scale(values):
    return lax.rsqrt(jnp.mean(values * values, axis=-1, keepdims=True) + EPS)


def silu_grads(act_grad, gate_val, up_val):
    gate_sigmoid = jax.nn.sigmoid(gate_val)
    gate_grad = act_grad * up_val * gate_sigmoid * (1.0 + gate_val * (1.0 - gate_sigmoid))
    up_grad = act_grad * (gate_val * gate_sigmoid)
    return (gate_grad, up_grad)


def from_facing(x):
    flip = lax.axis_size("ring") * 2 + 1
    count = 2 * lax.axis_size("ring") * 2
    return lax.ppermute(x, GRID, [(i, i ^ flip) for i in range(count)])


def swap(x):
    return lax.ppermute(x, "tensor", [(0, 1), (1, 0)])


def together(*arrays):
    return lax.optimization_barrier(arrays)


UNITS = 384
VMEM = 56 * 1024 * 1024


def feed_forward_kernel(h_ref, dy_ref, up_ref, down_ref, scale_ref, middle_ref, act_ref, dot_ref):
    routed = pl.program_id(0) < pl.num_programs(0) - 1
    tokens = h_ref.shape[0]
    step = 256

    @pl.when(pl.program_id(0) == 0)
    def _():
        dot_ref[...] = jnp.zeros_like(dot_ref)

    for at in range(0, tokens, step):
        here = pl.ds(at, step)
        gate_up = mm(h_ref[here, :], up_ref[...])
        back = mm(dy_ref[here, :], down_ref[...])
        gate, up = gate_up[:, :UNITS], gate_up[:, UNITS:]
        scale = jnp.where(routed, scale_ref[here, 0:1], scale_ref[here, 1:2])
        sigma = jax.nn.sigmoid(gate)
        silu = gate * sigma
        act = (silu * up).astype(BF).astype(F32)
        dots = jnp.sum(act * back, axis=1, keepdims=True)
        place = lax.broadcasted_iota(jnp.int32, (step, LANES), 1)
        place = place == jnp.where(routed, 0, 1)
        dot_ref[here, :] += jnp.where(place, dots, 0.0)
        back = back * scale
        act_ref[here, :] = (act * scale).astype(BF)
        middle_ref[here, :UNITS] = (back * up * sigma * (1.0 + gate * (1.0 - sigma))).astype(BF)
        middle_ref[here, UNITS:] = (back * silu).astype(BF)


def feed_forward(h, dy, weights, scales):
    tokens, width = h.shape
    parts = weights.shape[1] // (3 * UNITS)

    def whole(columns):
        return pl.BlockSpec((tokens, columns), lambda i: (0, 0), pipeline_mode=pl.Buffered(1))

    return pl.pallas_call(
        feed_forward_kernel,
        grid=(parts,),
        in_specs=[
            whole(width),
            whole(width),
            pl.BlockSpec((width, 2 * UNITS), lambda i: (0, i)),
            pl.BlockSpec((width, UNITS), lambda i: (0, 2 * parts + i)),
            whole(LANES),
        ],
        out_specs=[
            pl.BlockSpec((tokens, 2 * UNITS), lambda i: (0, i)),
            pl.BlockSpec((tokens, UNITS), lambda i: (0, i)),
            pl.BlockSpec((tokens, LANES), lambda i: (0, 0)),
        ],
        out_shape=[
            jax.ShapeDtypeStruct((tokens, 2 * UNITS * parts), BF),
            jax.ShapeDtypeStruct((tokens, UNITS * parts), BF),
            jax.ShapeDtypeStruct((tokens, LANES), F32),
        ],
        compiler_params=pltpu.CompilerParams(vmem_limit_bytes=VMEM),
    )(h, dy, weights, weights, scales)


def ffn_grads_kernel(h_ref, dy_ref, middle_ref, act_ref, grad_ref):
    ups = middle_ref.shape[1]
    grad_ref[:, :ups] = mm_tn(h_ref[...], middle_ref[...]).astype(BF)
    grad_ref[:, ups:] = mm_tn(dy_ref[...], act_ref[...]).astype(BF)


def ffn_grads(h, dy, middle, act):
    tokens, width = h.shape
    ups, downs = middle.shape[1], act.shape[1]
    step = 256
    return pl.pallas_call(
        ffn_grads_kernel,
        grid=(width // step,),
        in_specs=[
            pl.BlockSpec((tokens, step), lambda i: (0, i)),
            pl.BlockSpec((tokens, step), lambda i: (0, i)),
            pl.BlockSpec((tokens, ups), lambda i: (0, 0)),
            pl.BlockSpec((tokens, downs), lambda i: (0, 0)),
        ],
        out_specs=pl.BlockSpec((step, ups + downs), lambda i: (i, 0)),
        out_shape=jax.ShapeDtypeStruct((width, ups + downs), BF),
        compiler_params=pltpu.CompilerParams(vmem_limit_bytes=VMEM),
    )(h, dy, middle, act)


def attn_grads_kernel(h_ref, linear_ref, small_ref, dx_ref, heads_ref, grad_ref):
    qkv = linear_ref.shape[1]
    grad_ref[:, :qkv] = mm_tn(h_ref[...], linear_ref[...]).astype(BF)
    grad_ref[:, qkv : qkv + LANES] = small_ref[...].T.astype(BF)
    grad_ref[:, qkv + LANES :] = mm_tn(dx_ref[...], heads_ref[...]).astype(BF)


def attn_grads(h, linear, small, dx, heads):
    tokens, width = h.shape
    rows, heads_width = heads.shape
    qkv = linear.shape[1]
    columns = qkv + LANES + heads_width
    step = 256
    return pl.pallas_call(
        attn_grads_kernel,
        grid=(width // step,),
        in_specs=[
            pl.BlockSpec((tokens, step), lambda i: (0, i)),
            pl.BlockSpec((tokens, qkv), lambda i: (0, 0)),
            pl.BlockSpec((LANES, step), lambda i: (0, i)),
            pl.BlockSpec((rows, step), lambda i: (0, i)),
            pl.BlockSpec((rows, heads_width), lambda i: (0, 0)),
        ],
        out_specs=pl.BlockSpec((step, columns), lambda i: (i, 0)),
        out_shape=jax.ShapeDtypeStruct((width, columns), BF),
        compiler_params=pltpu.CompilerParams(vmem_limit_bytes=VMEM),
    )(h, linear, small, dx, heads)


def plane_gather(x):
    n, width = x.shape
    count = lax.axis_size(SEQ) * lax.axis_size("tensor")
    copies = jnp.broadcast_to(x[None], (count, n, width))
    return lax.all_to_all(copies, GRID, 0, 0, tiled=True).reshape(count * n, width)


def send_parts(parts):
    count = lax.axis_size(SEQ) * lax.axis_size("tensor")
    parts = parts.astype(BF).reshape(count, -1, parts.shape[-1])
    return lax.all_to_all(parts, GRID, 0, 0, tiled=True)


def sum_parts(parts):
    return jnp.sum(parts.astype(F32), axis=0)


def plane_scatter(parts):
    return sum_parts(send_parts(parts))


def body(
    hidden_in,
    grad_out,
    expert_ids,
    slot_rank,
    piece_start,
    norm_attn,
    w_qkv,
    b_qkv,
    w_proj,
    norm_ffn,
    w_router,
    w_share_gate,
    expert_gate_up,
    expert_down,
    shared_gate_up,
    shared_down,
):
    seqs = lax.axis_size(SEQ)
    dps = lax.axis_size("dp")
    me_seq = lax.axis_index(SEQ)
    me_tensor = lax.axis_index("tensor")
    me = me_seq * 2 + me_tensor
    rows = hidden_in.shape[1]
    own = rows // 2
    length = rows * seqs
    depth = w_qkv.shape[0]
    width = depth * dps * seqs
    experts = expert_gate_up.shape[1]
    fe = expert_gate_up.shape[3]
    fs = shared_gate_up.shape[2] // seqs
    fe_pad = up_to(fe, UNITS)
    fs_pad = up_to(fs, UNITS)
    bias_part = b_qkv.shape[2]
    heads = b_qkv.shape[1]
    capacity = (5 * rows * TOPK + 4 * experts - 1) // (4 * experts)
    score_scale = 1.0 / math.sqrt(HD)

    def mine(x):
        return lax.dynamic_slice_in_dim(x, me_tensor * own, own, 0)

    def both_halves(x):
        other = swap(x)
        first = jnp.where(me_tensor == 0, x, other)
        second = jnp.where(me_tensor == 0, other, x)
        return jnp.concatenate([first, second], 0)

    flat_ids = expert_ids[0].reshape(-1)
    flat_rank = slot_rank[0].reshape(-1)
    earlier = (flat_rank[None, :] < flat_rank[:, None]) & (flat_ids[None, :] == flat_ids[:, None])
    position = jnp.sum(earlier.astype(jnp.int32), axis=1)
    position = jnp.where(position < capacity, position, LANES - 1)
    chosen = expert_ids[0][:, :, None] == jnp.arange(experts, dtype=jnp.int32)[None, None, :]
    slot_of = jnp.sum(
        jnp.where(chosen, position.reshape(rows, TOPK)[:, :, None] - (LANES - 1), 0), axis=1
    ) + (LANES - 1)
    slot_cols = jnp.pad(slot_of.astype(BF), ((0, 0), (0, LANES - experts)))
    dy_own = mine(grad_out[0])
    dy_slots = jnp.concatenate([grad_out[0], slot_cols], 1)
    x_own = mine(hidden_in[0])

    misc = jnp.concatenate(
        [norm_attn[:, None], norm_ffn[:, None], w_share_gate[:, None], w_router], axis=1
    )
    n_misc = misc.shape[1]
    bias_rows = b_qkv.transpose(1, 0, 2).reshape(heads, 3 * bias_part)
    bias_rows = jnp.pad(bias_rows, ((0, 0), (0, depth - 3 * bias_part)))
    attn_blob = jnp.concatenate(
        [
            w_qkv.reshape(depth, 3, heads, HD).transpose(2, 0, 1, 3).reshape(heads, depth, 3 * HD),
            jnp.broadcast_to(misc[None], (heads, depth, n_misc)),
            bias_rows[:, :, None],
            jnp.zeros((heads, depth, LANES - n_misc - 1), BF),
        ],
        axis=2,
    )
    def padded(x, units):
        return jnp.pad(x, ((0, 0), (0, 0), (0, units - x.shape[2])))

    units = fe_pad + fs_pad
    egu_blob = expert_gate_up.transpose(1, 2, 0, 3)
    sgu_blob = shared_gate_up.reshape(depth, 2, seqs, fs).transpose(2, 1, 0, 3)
    edn_blob = expert_down.transpose(0, 2, 1)
    sdn_blob = shared_down.reshape(seqs, fs, depth).transpose(0, 2, 1)
    columns = []
    for blob, blob_units in ((egu_blob, fe_pad), (sgu_blob, fs_pad)):
        gates, ups = padded(blob[:, 0], blob_units), padded(blob[:, 1], blob_units)
        for at in range(0, blob_units, UNITS):
            columns += [gates[:, :, at : at + UNITS], ups[:, :, at : at + UNITS]]
    columns += [padded(edn_blob, fe_pad), padded(sdn_blob, fs_pad)]
    ffn_blob = jnp.concatenate(columns, axis=2)

    facing = from_facing(dy_slots)
    first_ring = lax.axis_index("z_hi") == 0
    dy_slots = jnp.stack(
        [jnp.where(first_ring, dy_slots, facing), jnp.where(first_ring, facing, dy_slots)]
    )

    x_all = plane_gather(x_own)
    proj_rows = lax.all_gather(w_proj.T, ("dp", *SEQ), axis=0, tiled=True)

    x_all, attn_blob = together(x_all, attn_blob)
    attn_blob = lax.all_to_all(attn_blob, SEQ, 0, 0, tiled=True).reshape(1, seqs * depth, -1)
    attn_full = jnp.broadcast_to(attn_blob, (dps, *attn_blob.shape[1:]))
    attn_full = lax.all_to_all(attn_full, "dp", 0, 0, tiled=True).reshape(width, -1)
    qkv_full = attn_full[:, : 3 * HD]
    misc_full = attn_full[:, 3 * HD :]

    attn_full, ffn_blob, dy_slots, proj_rows = together(attn_full, ffn_blob, dy_slots, proj_rows)
    dy_slots = lax.all_gather(dy_slots, "ring", axis=1, tiled=True)
    ffn_blob = lax.all_to_all(ffn_blob, SEQ, 0, 0, tiled=True)

    bias_full = misc_full[:, n_misc].reshape(dps * seqs, depth)[:, : 3 * bias_part]
    bias_full = bias_full.reshape(dps * seqs, 3, bias_part).transpose(1, 0, 2).reshape(1, 3 * HD)
    misc_rows = misc_full[:, :n_misc].T.astype(F32)
    gain_attn = misc_rows[0:1]
    gain_ffn = misc_rows[1:2]

    positions = jnp.arange(length, dtype=jnp.int32)
    freq_table = jnp.exp(jnp.arange(HD // 2, dtype=F32) * (-2.0 * math.log(THETA) / HD))
    angle = positions.astype(F32)[:, None] * freq_table[None, :]
    cosine = jnp.cos(angle)
    sine = jnp.sin(angle)
    starts = piece_start[0]
    inside = (positions[:, None] >= starts[None, :]) & (
        positions[:, None] < starts[None, :] + PIC
    )
    labels = jnp.arange(starts.shape[0], dtype=jnp.int32)
    segment = jnp.max(jnp.where(inside, labels[None, :], -1), axis=1)

    def seen():
        causal = positions[None, :] <= positions[:, None]
        picture = (segment[:, None] == segment[None, :]) & (segment[:, None] >= 0)
        return causal | picture

    def rotate(values):
        lead, tail = values[:, : HD // 2], values[:, HD // 2 :]
        return jnp.concatenate([lead * cosine - tail * sine, tail * cosine + lead * sine], axis=1)

    def unrotate(values):
        lead, tail = values[:, : HD // 2], values[:, HD // 2 :]
        return jnp.concatenate([lead * cosine + tail * sine, tail * cosine - lead * sine], axis=1)

    resid_all = x_all.astype(F32)
    norm_one = resid_all * rms_scale(resid_all)
    normed_one = (norm_one * gain_attn).astype(BF)
    linear = mm(normed_one, qkv_full) + bias_full.astype(F32)
    query = rotate(linear[:, :HD]).astype(BF)
    key = rotate(linear[:, HD : 2 * HD]).astype(BF)
    value = linear[:, 2 * HD :].astype(BF)
    scores = jnp.where(seen(), mm_nt(query, key) * score_scale, MASKED)
    exp_scores = jnp.exp(scores - jnp.max(scores, axis=1, keepdims=True))
    attn_probs = exp_scores / jnp.sum(exp_scores, axis=1, keepdims=True)
    probs_low = attn_probs.astype(BF)
    attn_head = mm(probs_low, value).astype(BF)

    by_head, ffn_blob = together(attn_head.reshape(seqs, rows, HD), ffn_blob)
    by_head = lax.all_to_all(by_head, SEQ, 0, 0, tiled=True)
    by_head, ffn_blob, dy_slots = together(by_head, ffn_blob, dy_slots)
    ffn_full = lax.all_gather(ffn_blob.reshape(seqs * depth, -1), "dp", axis=0, tiled=True)
    w_up = ffn_full[:, : 2 * units]
    w_down = ffn_full[:, 2 * units :]
    dy_slots = dy_slots.reshape(length, width + LANES)
    slots_all = dy_slots[:, width : width + experts].astype(jnp.int32)
    attn_flat = by_head.transpose(1, 0, 2).reshape(rows, heads * HD)
    attn_part = mm_nt(attn_flat, proj_rows)
    theirs = lax.dynamic_slice_in_dim(attn_part, (1 - me_tensor) * own, own, 0)
    attn_sum = mine(attn_part) + swap(theirs.astype(BF)).astype(F32)
    after_attn = x_own.astype(F32) + attn_sum
    scale_two = rms_scale(after_attn)
    norm_two = after_attn * scale_two
    normed_two = (norm_two * gain_ffn).astype(BF)
    h_all = plane_gather(normed_two)

    logits_all = mm(h_all, misc_full)
    router_probs = jax.nn.softmax(logits_all[:, 3 : 3 + experts], axis=-1)
    share_sig = jax.nn.sigmoid(logits_all[:, 2:3])
    mine_e = jnp.arange(experts, dtype=jnp.int32)[None, :] == me_seq
    slot_all = jnp.sum(jnp.where(mine_e, slots_all, 0), axis=1, keepdims=True)
    kept = slot_all < capacity
    gate_all = jnp.sum(jnp.where(mine_e, router_probs, 0.0), axis=1, keepdims=True)
    gate_all = jnp.where(kept, gate_all, 0.0)

    scales = jnp.pad(jnp.concatenate([gate_all, share_sig], 1), ((0, 0), (0, LANES - 2)))
    dgate_up, act_weighed, dots = feed_forward(h_all, dy_slots, ffn_full, scales)
    dots = jnp.concatenate([jnp.where(mine_e & kept, dots[:, 0:1], 0.0), dots[:, 1:2]], 1)
    dots = jnp.pad(dots, ((0, 0), (0, LANES - experts - 1)))
    back_parts = jnp.concatenate([mm_nt(dgate_up, w_up).astype(BF), dots.astype(BF)], 1)
    back_parts, act_weighed, dgate_up = together(back_parts, act_weighed, dgate_up)
    back = send_parts(back_parts)

    ffn_grad = ffn_grads(h_all, dy_slots, dgate_up, act_weighed)
    ffn_parts = mm_nt(act_weighed, w_down).astype(BF)
    back, ffn_parts, ffn_grad = together(back, ffn_parts, ffn_grad)
    back = sum_parts(back)
    ffn_grad = lax.psum_scatter(ffn_grad, "dp", scatter_dimension=0, tiled=True)

    probs_own = lax.dynamic_slice_in_dim(router_probs, me * own, own, 0)
    sig_own = lax.dynamic_slice_in_dim(share_sig, me * own, own, 0)
    dprobs = back[:, width : width + experts]
    dlogits = probs_own * (dprobs - jnp.sum(probs_own * dprobs, axis=1, keepdims=True))
    dshare = back[:, width + experts : width + experts + 1] * sig_own * (1.0 - sig_own)
    dmisc = jnp.concatenate([jnp.zeros((own, 2), F32), dshare, dlogits], 1)
    dmisc = jnp.pad(dmisc, ((0, 0), (0, LANES - n_misc))).astype(BF)
    dh_two = back[:, :width] + mm_nt(dmisc, misc_full)
    grad_misc = mm_tn(dmisc, normed_two)
    grad_gain_ffn = jnp.sum(dh_two * norm_two, axis=0)
    inner_two = dh_two * gain_ffn
    dx_one = dy_own.astype(F32) + scale_two * (
        inner_two - norm_two * jnp.mean(inner_two * norm_two, axis=-1, keepdims=True)
    )
    dx_low = dx_one.astype(BF)

    dx_pair = both_halves(dx_low)
    do_flat = mm(dx_pair, proj_rows).astype(BF)
    do_heads = do_flat.reshape(rows, heads, HD).transpose(1, 0, 2)
    do_head = lax.all_to_all(do_heads, SEQ, 0, 0, tiled=True).reshape(length, HD)
    dvalue = mm_tn(probs_low, do_head)
    dprob = mm_nt(do_head, value)
    row_delta = jnp.sum(attn_probs * dprob, axis=1, keepdims=True)
    dscore = (attn_probs * (dprob - row_delta)).astype(BF)
    dquery = mm(dscore, key) * score_scale
    dkey = mm_tn(dscore, query) * score_scale
    dlinear = jnp.concatenate([unrotate(dquery), unrotate(dkey), dvalue], 1).astype(BF)
    grad_bias = jnp.sum(dlinear.astype(F32), axis=0)
    dh_part = mm_nt(dlinear, qkv_full)
    grad_gain_attn = jnp.sum(dh_part * norm_one, axis=0)
    dh_sent = send_parts(dh_part)
    dh_sent, dlinear, ffn_parts, ffn_grad = together(dh_sent, dlinear, ffn_parts, ffn_grad)
    dh_one = sum_parts(dh_sent)

    bias_rows = grad_bias.reshape(3, dps * seqs, bias_part).transpose(1, 0, 2)
    bias_rows = bias_rows.reshape(dps * seqs, 3 * bias_part)
    bias_rows = jnp.pad(bias_rows, ((0, 0), (0, depth - 3 * bias_part))).reshape(1, width)
    small = jnp.concatenate(
        [grad_gain_attn[None], grad_gain_ffn[None], grad_misc[2:n_misc], bias_rows], 0
    )
    small = jnp.pad(small, ((0, LANES - n_misc - 1), (0, 0)))
    attn_grad = attn_grads(normed_one, dlinear, small, dx_pair, attn_flat)
    attn_grad = lax.psum_scatter(attn_grad, "dp", scatter_dimension=0, tiled=True)
    resid = x_own.astype(F32)
    scale_one = rms_scale(resid)
    norm_own = resid * scale_one
    inner_one = dh_one * gain_attn
    grad_in = dx_one + scale_one * (
        inner_one - norm_own * jnp.mean(inner_one * norm_own, axis=-1, keepdims=True)
    )
    grad_in = both_halves(grad_in)
    grad_in, ffn_grad = together(grad_in, ffn_grad)
    ffn_grad = lax.all_to_all(ffn_grad.reshape(seqs, depth, -1), SEQ, 0, 0, tiled=True)
    ffn_grad, ffn_parts = together(ffn_grad, ffn_parts)
    ffn_parts = send_parts(ffn_parts)
    ffn_parts, attn_grad = together(ffn_parts, attn_grad)
    hidden_out = both_halves((after_attn + sum_parts(ffn_parts)).astype(BF))
    attn_grad = attn_grad.reshape(seqs, depth, -1)
    attn_grad = lax.all_to_all(attn_grad, SEQ, 0, 0, tiled=True).astype(F32)

    def unit_columns(first, kind, size):
        at = [(2 * (first + i) + kind) * UNITS for i in range(up_to(size, UNITS) // UNITS)]
        picked = [
            ffn_grad[:, :, c : c + min(UNITS, size - i * UNITS)] for i, c in enumerate(at)
        ]
        return jnp.concatenate(picked, 2).astype(F32)

    shared_at = fe_pad // UNITS
    out_egu = jnp.stack([unit_columns(0, 0, fe), unit_columns(0, 1, fe)], 2).transpose(1, 0, 2, 3)
    out_sgu = [unit_columns(shared_at, kind, fs).transpose(1, 0, 2) for kind in (0, 1)]
    out_sgu = jnp.stack(out_sgu, 1).reshape(depth, 2, seqs * fs)
    down_at = 2 * units
    out_edn = ffn_grad[:, :, down_at : down_at + fe].transpose(0, 2, 1).astype(F32)
    out_sdn = ffn_grad[:, :, down_at + fe_pad : down_at + fe_pad + fs].transpose(0, 2, 1)
    out_sdn = out_sdn.reshape(seqs * fs, depth).astype(F32)
    out_qkv = attn_grad[:, :, : 3 * HD].reshape(heads, depth, 3, HD)
    out_qkv = out_qkv.transpose(1, 2, 0, 3).reshape(depth, 3, heads * HD)
    out_misc = jnp.sum(attn_grad[:, :, 3 * HD : 3 * HD + n_misc], axis=0)
    out_misc = out_misc + swap(out_misc)
    out_bias = attn_grad[:, : 3 * bias_part, 3 * HD + n_misc]
    out_bias = out_bias.reshape(heads, 3, bias_part).transpose(1, 0, 2)
    out_proj = jnp.sum(attn_grad[:, :, 3 * HD + LANES :], axis=0).T

    return (
        hidden_out[None],
        grad_in[None],
        out_misc[:, 0],
        out_qkv,
        out_bias,
        out_proj,
        out_misc[:, 1],
        out_misc[:, 3:n_misc],
        out_misc[:, 2],
        out_egu,
        out_edn,
        out_sgu,
        out_sdn,
    )


def solution(mesh):
    in_specs = (
        P("dp", SEQ, None),
        P("dp", SEQ, None),
        P("dp", SEQ, None),
        P("dp", SEQ, None),
        P("dp", None),
        P(("dp", *SEQ)),
        P(("dp", *SEQ), None, "tensor"),
        P(None, "tensor", ("dp", *SEQ)),
        P("tensor", ("dp", *SEQ)),
        P(("dp", *SEQ)),
        P(("dp", *SEQ), None),
        P(("dp", *SEQ)),
        P(("dp", *SEQ), None, None, "tensor"),
        P(None, "tensor", ("dp", *SEQ)),
        P(("dp", *SEQ), None, "tensor"),
        P("tensor", ("dp", *SEQ)),
    )
    out_specs = (
        P("dp", SEQ, None),
        P("dp", SEQ, None),
        P(("dp", *SEQ)),
        P(("dp", *SEQ), None, "tensor"),
        P(None, "tensor", ("dp", *SEQ)),
        P("tensor", ("dp", *SEQ)),
        P(("dp", *SEQ)),
        P(("dp", *SEQ), None),
        P(("dp", *SEQ)),
        P(("dp", *SEQ), None, None, "tensor"),
        P(None, "tensor", ("dp", *SEQ)),
        P(("dp", *SEQ), None, "tensor"),
        P("tensor", ("dp", *SEQ)),
    )
    fine = Mesh(mesh.devices.reshape(mesh.shape["dp"], 2, -1, 2), ("dp", *SEQ, "tensor"))
    return jax.shard_map(body, mesh=fine, in_specs=in_specs, out_specs=out_specs, check_vma=False)
```

```python
import functools
import math

import jax
import jax.numpy as jnp
from jax import lax
from jax.experimental import pallas as pl
from jax.experimental.pallas import tpu as pltpu
from jax.sharding import Mesh
from jax.sharding import PartitionSpec as P

HD = 128
TOPK = 4
PIC = 256

EPS = 1e-06
THETA = 1000000.0
MASKED = -1000000000.0

SEQ = ("z_hi", "ring")
GRID = ("z_hi", "ring", "tensor")
BF = jnp.bfloat16
F32 = jnp.float32
LANES = 128


def up_to(size, multiple):
    return -(-size // multiple) * multiple


def dot(a, b, dims):
    return lax.dot_general(a, b, (dims, ((), ())), preferred_element_type=F32)


def mm(a, b):
    return dot(a, b, ((1,), (0,)))


def mm_nt(a, b):
    return dot(a, b, ((1,), (1,)))


def mm_tn(a, b):
    return dot(a, b, ((0,), (0,)))


def rms_scale(values):
    return lax.rsqrt(jnp.mean(values * values, axis=-1, keepdims=True) + EPS)


def silu_grads(act_grad, gate_val, up_val):
    gate_sigmoid = jax.nn.sigmoid(gate_val)
    gate_grad = act_grad * up_val * gate_sigmoid * (1.0 + gate_val * (1.0 - gate_sigmoid))
    up_grad = act_grad * (gate_val * gate_sigmoid)
    return (gate_grad, up_grad)


def from_facing(x):
    flip = lax.axis_size("ring") * 2 + 1
    count = 2 * lax.axis_size("ring") * 2
    return lax.ppermute(x, GRID, [(i, i ^ flip) for i in range(count)])


def swap(x):
    return lax.ppermute(x, "tensor", [(0, 1), (1, 0)])


def together(*arrays):
    return lax.optimization_barrier(arrays)


UNITS = 384
EXPERTS = 8
SHARE_AT = 2
EXPERT_AT = 3
VMEM = 56 * 1024 * 1024


def feed_forward_kernel(
    capacity, expert_ref, h_ref, dy_ref, up_ref, down_ref, misc_ref,
    middle_ref, act_ref, dot_ref, prob_ref, scale_ref,
):
    part = pl.program_id(0)
    routed = part < pl.num_programs(0) - 1
    tokens, width = h_ref.shape
    expert = expert_ref[0]
    step = 256
    lane = lax.broadcasted_iota(jnp.int32, (step, LANES), 1)

    def column(x, at):
        return jnp.sum(jnp.where(lane == at, x, 0.0), axis=1, keepdims=True)

    @pl.when(part == 0)
    def _():
        for at in range(0, tokens, step):
            here = pl.ds(at, step)
            logits = mm(h_ref[here, :], misc_ref[...])
            among = (lane >= EXPERT_AT) & (lane < EXPERT_AT + EXPERTS)
            top = jnp.max(jnp.where(among, logits, -jnp.inf), axis=1, keepdims=True)
            raised = jnp.where(among, jnp.exp(jnp.where(among, logits - top, 0.0)), 0.0)
            probs = raised / jnp.sum(raised, axis=1, keepdims=True)
            share = jax.nn.sigmoid(column(logits, SHARE_AT))
            slot = column(dy_ref[here, width:].astype(F32), expert)
            gate = jnp.where(slot < capacity, column(probs, EXPERT_AT + expert), 0.0)
            prob_ref[here, :] = jnp.where(lane == SHARE_AT, share, probs)
            kept = jnp.where(slot < capacity, 1.0, 0.0)
            scale_ref[here, :] = jnp.where(
                lane == 0, gate, jnp.where(lane == 1, share, jnp.where(lane == 2, kept, 0.0))
            )
        dot_ref[...] = jnp.zeros_like(dot_ref)

    for at in range(0, tokens, step):
        here = pl.ds(at, step)
        gate_up = mm(h_ref[here, :], up_ref[...])
        back = mm(dy_ref[here, :width], down_ref[...])
        gate, up = gate_up[:, :UNITS], gate_up[:, UNITS:]
        scale = jnp.where(routed, scale_ref[here, 0:1], scale_ref[here, 1:2])
        counts = jnp.where(routed, scale_ref[here, 2:3], 1.0)
        sigma = jax.nn.sigmoid(gate)
        silu = gate * sigma
        act = (silu * up).astype(BF).astype(F32)
        dots = jnp.sum(act * back, axis=1, keepdims=True) * counts
        dot_ref[here, :] += jnp.where(lane == jnp.where(routed, expert, EXPERTS), dots, 0.0)
        back = back * scale
        act_ref[here, :] = (act * scale).astype(BF)
        middle_ref[here, :UNITS] = (back * up * sigma * (1.0 + gate * (1.0 - sigma))).astype(BF)
        middle_ref[here, UNITS:] = (back * silu).astype(BF)


def feed_forward(h, others, weights, misc, expert, capacity):
    tokens, width = h.shape
    parts = weights.shape[1] // (3 * UNITS)

    def whole(shape):
        return pl.BlockSpec(shape, lambda i, e: (0, 0), pipeline_mode=pl.Buffered(1))

    return pl.pallas_call(
        functools.partial(feed_forward_kernel, capacity),
        grid_spec=pltpu.PrefetchScalarGridSpec(
            num_scalar_prefetch=1,
            grid=(parts,),
            in_specs=[
                whole(h.shape),
                whole((tokens, width + LANES)),
                pl.BlockSpec((width, 2 * UNITS), lambda i, e: (0, i)),
                pl.BlockSpec((width, UNITS), lambda i, e: (0, 2 * parts + i)),
                whole(misc.shape),
            ],
            out_specs=[
                pl.BlockSpec((tokens, 2 * UNITS), lambda i, e: (0, i)),
                pl.BlockSpec((tokens, UNITS), lambda i, e: (0, i)),
                pl.BlockSpec((tokens, LANES), lambda i, e: (0, 0)),
                pl.BlockSpec((tokens, LANES), lambda i, e: (0, 0)),
            ],
            scratch_shapes=[pltpu.VMEM((tokens, LANES), F32)],
        ),
        out_shape=[
            jax.ShapeDtypeStruct((tokens, 2 * UNITS * parts), BF),
            jax.ShapeDtypeStruct((tokens, UNITS * parts), BF),
            jax.ShapeDtypeStruct((tokens, LANES), F32),
            jax.ShapeDtypeStruct((tokens, LANES), F32),
        ],
        compiler_params=pltpu.CompilerParams(vmem_limit_bytes=VMEM),
    )(expert, h, others, weights, weights, misc)


def ffn_rest_kernel(h_ref, dy_ref, middle_ref, act_ref, down_ref, grad_ref, out_ref):
    ups = middle_ref.shape[1]
    grad_ref[:, :ups] = mm_tn(h_ref[...], middle_ref[...]).astype(BF)
    grad_ref[:, ups:] = mm_tn(dy_ref[...], act_ref[...]).astype(BF)
    out_ref[...] = mm_nt(act_ref[...], down_ref[...]).astype(BF)


def ffn_rest(h, dy, middle, act, weights):
    tokens, width = h.shape
    ups, downs = middle.shape[1], act.shape[1]
    step = 256
    return pl.pallas_call(
        ffn_rest_kernel,
        grid=(width // step,),
        in_specs=[
            pl.BlockSpec((tokens, step), lambda i: (0, i)),
            pl.BlockSpec((tokens, step), lambda i: (0, i)),
            pl.BlockSpec((tokens, ups), lambda i: (0, 0)),
            pl.BlockSpec((tokens, downs), lambda i: (0, 0)),
            pl.BlockSpec((step, downs), lambda i: (i, ups // downs)),
        ],
        out_specs=[
            pl.BlockSpec((step, ups + downs), lambda i: (i, 0)),
            pl.BlockSpec((tokens, step), lambda i: (0, i)),
        ],
        out_shape=[
            jax.ShapeDtypeStruct((width, ups + downs), BF),
            jax.ShapeDtypeStruct((tokens, width), BF),
        ],
        compiler_params=pltpu.CompilerParams(vmem_limit_bytes=VMEM),
    )(h, dy, middle, act, weights)


def attn_grads_kernel(h_ref, linear_ref, small_ref, dx_ref, heads_ref, grad_ref):
    qkv = linear_ref.shape[1]
    grad_ref[:, :qkv] = mm_tn(h_ref[...], linear_ref[...]).astype(BF)
    grad_ref[:, qkv : qkv + LANES] = small_ref[...].T.astype(BF)
    grad_ref[:, qkv + LANES :] = mm_tn(dx_ref[...], heads_ref[...]).astype(BF)


def attn_grads(h, linear, small, dx, heads):
    tokens, width = h.shape
    rows, heads_width = heads.shape
    qkv = linear.shape[1]
    columns = qkv + LANES + heads_width
    step = 256
    return pl.pallas_call(
        attn_grads_kernel,
        grid=(width // step,),
        in_specs=[
            pl.BlockSpec((tokens, step), lambda i: (0, i)),
            pl.BlockSpec((tokens, qkv), lambda i: (0, 0)),
            pl.BlockSpec((LANES, step), lambda i: (0, i)),
            pl.BlockSpec((rows, step), lambda i: (0, i)),
            pl.BlockSpec((rows, heads_width), lambda i: (0, 0)),
        ],
        out_specs=pl.BlockSpec((step, columns), lambda i: (i, 0)),
        out_shape=jax.ShapeDtypeStruct((width, columns), BF),
        compiler_params=pltpu.CompilerParams(vmem_limit_bytes=VMEM),
    )(h, linear, small, dx, heads)


def plane_gather(x):
    n, width = x.shape
    count = lax.axis_size(SEQ) * lax.axis_size("tensor")
    copies = jnp.broadcast_to(x[None], (count, n, width))
    return lax.all_to_all(copies, GRID, 0, 0, tiled=True).reshape(count * n, width)


def send_parts(parts):
    count = lax.axis_size(SEQ) * lax.axis_size("tensor")
    parts = parts.astype(BF).reshape(count, -1, parts.shape[-1])
    return lax.all_to_all(parts, GRID, 0, 0, tiled=True)


def sum_parts(parts):
    return jnp.sum(parts.astype(F32), axis=0)


def plane_scatter(parts):
    return sum_parts(send_parts(parts))


def body(
    hidden_in,
    grad_out,
    expert_ids,
    slot_rank,
    piece_start,
    norm_attn,
    w_qkv,
    b_qkv,
    w_proj,
    norm_ffn,
    w_router,
    w_share_gate,
    expert_gate_up,
    expert_down,
    shared_gate_up,
    shared_down,
):
    seqs = lax.axis_size(SEQ)
    dps = lax.axis_size("dp")
    me_seq = lax.axis_index(SEQ)
    me_tensor = lax.axis_index("tensor")
    me = me_seq * 2 + me_tensor
    rows = hidden_in.shape[1]
    own = rows // 2
    length = rows * seqs
    depth = w_qkv.shape[0]
    width = depth * dps * seqs
    experts = expert_gate_up.shape[1]
    fe = expert_gate_up.shape[3]
    fs = shared_gate_up.shape[2] // seqs
    fe_pad = up_to(fe, UNITS)
    fs_pad = up_to(fs, UNITS)
    bias_part = b_qkv.shape[2]
    heads = b_qkv.shape[1]
    capacity = (5 * rows * TOPK + 4 * experts - 1) // (4 * experts)
    score_scale = 1.0 / math.sqrt(HD)

    def mine(x):
        return lax.dynamic_slice_in_dim(x, me_tensor * own, own, 0)

    def both_halves(x):
        other = swap(x)
        first = jnp.where(me_tensor == 0, x, other)
        second = jnp.where(me_tensor == 0, other, x)
        return jnp.concatenate([first, second], 0)

    flat_ids = expert_ids[0].reshape(-1)
    flat_rank = slot_rank[0].reshape(-1)
    earlier = (flat_rank[None, :] < flat_rank[:, None]) & (flat_ids[None, :] == flat_ids[:, None])
    position = jnp.sum(earlier.astype(jnp.int32), axis=1)
    position = jnp.where(position < capacity, position, LANES - 1)
    chosen = expert_ids[0][:, :, None] == jnp.arange(experts, dtype=jnp.int32)[None, None, :]
    slot_of = jnp.sum(
        jnp.where(chosen, position.reshape(rows, TOPK)[:, :, None] - (LANES - 1), 0), axis=1
    ) + (LANES - 1)
    slot_cols = jnp.pad(mine(slot_of).astype(BF), ((0, 0), (0, LANES - experts)))
    dy_own = mine(grad_out[0])
    x_own = mine(hidden_in[0])

    misc = jnp.concatenate(
        [norm_attn[:, None], norm_ffn[:, None], w_share_gate[:, None], w_router], axis=1
    )
    n_misc = misc.shape[1]
    bias_rows = b_qkv.transpose(1, 0, 2).reshape(heads, 3 * bias_part)
    bias_rows = jnp.pad(bias_rows, ((0, 0), (0, depth - 3 * bias_part)))
    attn_blob = jnp.concatenate(
        [
            w_qkv.reshape(depth, 3, heads, HD).transpose(2, 0, 1, 3).reshape(heads, depth, 3 * HD),
            jnp.broadcast_to(misc[None], (heads, depth, n_misc)),
            bias_rows[:, :, None],
            jnp.zeros((heads, depth, LANES - n_misc - 1), BF),
        ],
        axis=2,
    )
    def padded(x, units):
        return jnp.pad(x, ((0, 0), (0, 0), (0, units - x.shape[2])))

    units = fe_pad + fs_pad
    egu_blob = expert_gate_up.transpose(1, 2, 0, 3)
    sgu_blob = shared_gate_up.reshape(depth, 2, seqs, fs).transpose(2, 1, 0, 3)
    edn_blob = expert_down.transpose(0, 2, 1)
    sdn_blob = shared_down.reshape(seqs, fs, depth).transpose(0, 2, 1)
    columns = []
    for blob, blob_units in ((egu_blob, fe_pad), (sgu_blob, fs_pad)):
        gates, ups = padded(blob[:, 0], blob_units), padded(blob[:, 1], blob_units)
        for at in range(0, blob_units, UNITS):
            columns += [gates[:, :, at : at + UNITS], ups[:, :, at : at + UNITS]]
    columns += [padded(edn_blob, fe_pad), padded(sdn_blob, fs_pad)]
    ffn_blob = jnp.concatenate(columns, axis=2)

    first_ring = lax.axis_index("z_hi") == 0

    def both_rings(block):
        facing = from_facing(block)
        return jnp.stack(
            [jnp.where(first_ring, block, facing), jnp.where(first_ring, facing, block)]
        )

    x_all = lax.all_gather(both_rings(hidden_in[0]), "ring", axis=1, tiled=True)
    x_all = x_all.reshape(length, width)

    attn_blob = lax.all_to_all(attn_blob, SEQ, 0, 0, tiled=True).reshape(1, seqs * depth, -1)
    attn_full = jnp.broadcast_to(attn_blob, (dps, *attn_blob.shape[1:]))
    attn_full = lax.all_to_all(attn_full, "dp", 0, 0, tiled=True).reshape(width, -1)
    x_all, attn_full, proj_rows, dy_slots = together(
        x_all, attn_full, w_proj.T, jnp.concatenate([dy_own, slot_cols], 1)
    )
    proj_rows = lax.all_gather(proj_rows, ("dp", *SEQ), axis=0, tiled=True)
    qkv_full = attn_full[:, : 3 * HD]
    misc_full = attn_full[:, 3 * HD :]
    dy_slots = plane_gather(dy_slots)

    bias_full = misc_full[:, n_misc].reshape(dps * seqs, depth)[:, : 3 * bias_part]
    bias_full = bias_full.reshape(dps * seqs, 3, bias_part).transpose(1, 0, 2).reshape(1, 3 * HD)
    misc_rows = misc_full[:, :n_misc].T.astype(F32)
    gain_attn = misc_rows[0:1]
    gain_ffn = misc_rows[1:2]

    positions = jnp.arange(length, dtype=jnp.int32)
    freq_table = jnp.exp(jnp.arange(HD // 2, dtype=F32) * (-2.0 * math.log(THETA) / HD))
    angle = positions.astype(F32)[:, None] * freq_table[None, :]
    cosine = jnp.cos(angle)
    sine = jnp.sin(angle)
    starts = piece_start[0]
    inside = (positions[:, None] >= starts[None, :]) & (
        positions[:, None] < starts[None, :] + PIC
    )
    labels = jnp.arange(starts.shape[0], dtype=jnp.int32)
    segment = jnp.max(jnp.where(inside, labels[None, :], -1), axis=1)

    def seen():
        causal = positions[None, :] <= positions[:, None]
        picture = (segment[:, None] == segment[None, :]) & (segment[:, None] >= 0)
        return causal | picture

    def rotate(values):
        lead, tail = values[:, : HD // 2], values[:, HD // 2 :]
        return jnp.concatenate([lead * cosine - tail * sine, tail * cosine + lead * sine], axis=1)

    def unrotate(values):
        lead, tail = values[:, : HD // 2], values[:, HD // 2 :]
        return jnp.concatenate([lead * cosine + tail * sine, tail * cosine - lead * sine], axis=1)

    resid_all = x_all.astype(F32)
    norm_one = resid_all * rms_scale(resid_all)
    normed_one = (norm_one * gain_attn).astype(BF)
    linear = mm(normed_one, qkv_full) + bias_full.astype(F32)
    query = rotate(linear[:, :HD]).astype(BF)
    key = rotate(linear[:, HD : 2 * HD]).astype(BF)
    value = linear[:, 2 * HD :].astype(BF)
    scores = jnp.where(seen(), mm_nt(query, key) * score_scale, MASKED)
    exp_scores = jnp.exp(scores - jnp.max(scores, axis=1, keepdims=True))
    attn_probs = exp_scores / jnp.sum(exp_scores, axis=1, keepdims=True)
    probs_low = attn_probs.astype(BF)
    attn_head = mm(probs_low, value).astype(BF)

    by_head, dy_slots = together(attn_head.reshape(seqs, rows, HD), dy_slots)
    by_head = lax.all_to_all(by_head, SEQ, 0, 0, tiled=True)
    by_head, ffn_blob = together(by_head, ffn_blob)
    ffn_blob = lax.all_to_all(ffn_blob, SEQ, 0, 0, tiled=True)
    attn_flat = by_head.transpose(1, 0, 2).reshape(rows, heads * HD)
    attn_part = mm_nt(attn_flat, proj_rows)
    theirs = lax.dynamic_slice_in_dim(attn_part, (1 - me_tensor) * own, own, 0)
    attn_sum = mine(attn_part) + swap(theirs.astype(BF)).astype(F32)
    after_attn = x_own.astype(F32) + attn_sum
    scale_two = rms_scale(after_attn)
    norm_two = after_attn * scale_two
    normed_two = (norm_two * gain_ffn).astype(BF)
    normed_sent, ffn_blob = together(normed_two, ffn_blob)
    ffn_full = lax.all_gather(ffn_blob.reshape(seqs * depth, -1), "dp", axis=0, tiled=True)
    w_up = ffn_full[:, : 2 * units]
    h_all = plane_gather(normed_sent)

    expert = me_seq.astype(jnp.int32).reshape(1)
    dgate_up, act_weighed, dots, router = feed_forward(
        h_all, dy_slots, ffn_full, misc_full, expert, capacity
    )
    back_parts = jnp.concatenate([mm_nt(dgate_up, w_up).astype(BF), dots.astype(BF)], 1)
    back_parts, act_weighed, dgate_up = together(back_parts, act_weighed, dgate_up)
    back = send_parts(back_parts)

    ffn_grad, ffn_parts = ffn_rest(h_all, dy_slots, dgate_up, act_weighed, ffn_full)
    back, ffn_parts, ffn_grad = together(back, ffn_parts, ffn_grad)
    back = sum_parts(back)
    ffn_grad = lax.psum_scatter(ffn_grad, "dp", scatter_dimension=0, tiled=True)
    half = width // 2
    ffn_left, ffn_right = ffn_parts[:, :half], ffn_parts[:, half:]

    router_own = lax.dynamic_slice_in_dim(router, me * own, own, 0)
    probs_own = router_own[:, EXPERT_AT : EXPERT_AT + experts]
    sig_own = router_own[:, SHARE_AT : SHARE_AT + 1]
    dprobs = back[:, width : width + experts]
    dlogits = probs_own * (dprobs - jnp.sum(probs_own * dprobs, axis=1, keepdims=True))
    dshare = back[:, width + experts : width + experts + 1] * sig_own * (1.0 - sig_own)
    dmisc = jnp.concatenate([jnp.zeros((own, 2), F32), dshare, dlogits], 1)
    dmisc = jnp.pad(dmisc, ((0, 0), (0, LANES - n_misc))).astype(BF)
    dh_two = back[:, :width] + mm_nt(dmisc, misc_full)
    grad_misc = mm_tn(dmisc, normed_two)
    grad_gain_ffn = jnp.sum(dh_two * norm_two, axis=0)
    inner_two = dh_two * gain_ffn
    dx_one = dy_own.astype(F32) + scale_two * (
        inner_two - norm_two * jnp.mean(inner_two * norm_two, axis=-1, keepdims=True)
    )
    dx_low = dx_one.astype(BF)

    dx_pair = both_halves(dx_low)
    do_flat = mm(dx_pair, proj_rows).astype(BF)
    do_heads = do_flat.reshape(rows, heads, HD).transpose(1, 0, 2)
    do_head = lax.all_to_all(do_heads, SEQ, 0, 0, tiled=True).reshape(length, HD)
    do_head, ffn_left = together(do_head, ffn_left)
    ffn_left = send_parts(ffn_left)
    dvalue = mm_tn(probs_low, do_head)
    dprob = mm_nt(do_head, value)
    row_delta = jnp.sum(attn_probs * dprob, axis=1, keepdims=True)
    dscore = (attn_probs * (dprob - row_delta)).astype(BF)
    dquery = mm(dscore, key) * score_scale
    dkey = mm_tn(dscore, query) * score_scale
    dlinear = jnp.concatenate([unrotate(dquery), unrotate(dkey), dvalue], 1).astype(BF)
    grad_bias = jnp.sum(dlinear.astype(F32), axis=0)
    dh_part = mm_nt(dlinear, qkv_full)
    grad_gain_attn = jnp.sum(dh_part * norm_one, axis=0)
    dh_low, ffn_left = together(dh_part.astype(BF), ffn_left)
    dh_sent = send_parts(dh_low)

    bias_rows = grad_bias.reshape(3, dps * seqs, bias_part).transpose(1, 0, 2)
    bias_rows = bias_rows.reshape(dps * seqs, 3 * bias_part)
    bias_rows = jnp.pad(bias_rows, ((0, 0), (0, depth - 3 * bias_part))).reshape(1, width)
    small = jnp.concatenate(
        [grad_gain_attn[None], grad_gain_ffn[None], grad_misc[2:n_misc], bias_rows], 0
    )
    small = jnp.pad(small, ((0, LANES - n_misc - 1), (0, 0)))
    attn_grad = attn_grads(normed_one, dlinear, small, dx_pair, attn_flat)
    dh_sent, attn_grad, ffn_grad = together(dh_sent, attn_grad, ffn_grad)
    attn_grad = lax.psum_scatter(attn_grad, "dp", scatter_dimension=0, tiled=True)
    dh_one = sum_parts(dh_sent)
    resid = x_own.astype(F32)
    scale_one = rms_scale(resid)
    norm_own = resid * scale_one
    inner_one = dh_one * gain_attn
    grad_in = dx_one + scale_one * (
        inner_one - norm_own * jnp.mean(inner_one * norm_own, axis=-1, keepdims=True)
    )
    grad_in = both_halves(grad_in)
    ffn_grad = lax.all_to_all(ffn_grad.reshape(seqs, depth, -1), SEQ, 0, 0, tiled=True)
    ffn_grad, ffn_right = together(ffn_grad, ffn_right)
    ffn_right = send_parts(ffn_right)
    ffn_right, attn_grad, grad_in = together(ffn_right, attn_grad, grad_in)
    ffn_sum = jnp.concatenate([sum_parts(ffn_left), sum_parts(ffn_right)], 1)
    hidden_out = both_halves((after_attn + ffn_sum).astype(BF))
    attn_grad = attn_grad.reshape(seqs, depth, -1)
    attn_grad = lax.all_to_all(attn_grad, SEQ, 0, 0, tiled=True).astype(F32)

    def unit_columns(first, kind, size):
        at = [(2 * (first + i) + kind) * UNITS for i in range(up_to(size, UNITS) // UNITS)]
        picked = [
            ffn_grad[:, :, c : c + min(UNITS, size - i * UNITS)] for i, c in enumerate(at)
        ]
        return jnp.concatenate(picked, 2).astype(F32)

    shared_at = fe_pad // UNITS
    out_egu = jnp.stack([unit_columns(0, 0, fe), unit_columns(0, 1, fe)], 2).transpose(1, 0, 2, 3)
    out_sgu = [unit_columns(shared_at, kind, fs).transpose(1, 0, 2) for kind in (0, 1)]
    out_sgu = jnp.stack(out_sgu, 1).reshape(depth, 2, seqs * fs)
    down_at = 2 * units
    out_edn = ffn_grad[:, :, down_at : down_at + fe].transpose(0, 2, 1).astype(F32)
    out_sdn = ffn_grad[:, :, down_at + fe_pad : down_at + fe_pad + fs].transpose(0, 2, 1)
    out_sdn = out_sdn.reshape(seqs * fs, depth).astype(F32)
    out_qkv = attn_grad[:, :, : 3 * HD].reshape(heads, depth, 3, HD)
    out_qkv = out_qkv.transpose(1, 2, 0, 3).reshape(depth, 3, heads * HD)
    out_misc = jnp.sum(attn_grad[:, :, 3 * HD : 3 * HD + n_misc], axis=0)
    out_misc = out_misc + swap(out_misc)
    out_bias = attn_grad[:, : 3 * bias_part, 3 * HD + n_misc]
    out_bias = out_bias.reshape(heads, 3, bias_part).transpose(1, 0, 2)
    out_proj = jnp.sum(attn_grad[:, :, 3 * HD + LANES :], axis=0).T

    return (
        hidden_out[None],
        grad_in[None],
        out_misc[:, 0],
        out_qkv,
        out_bias,
        out_proj,
        out_misc[:, 1],
        out_misc[:, 3:n_misc],
        out_misc[:, 2],
        out_egu,
        out_edn,
        out_sgu,
        out_sdn,
    )


def solution(mesh):
    in_specs = (
        P("dp", SEQ, None),
        P("dp", SEQ, None),
        P("dp", SEQ, None),
        P("dp", SEQ, None),
        P("dp", None),
        P(("dp", *SEQ)),
        P(("dp", *SEQ), None, "tensor"),
        P(None, "tensor", ("dp", *SEQ)),
        P("tensor", ("dp", *SEQ)),
        P(("dp", *SEQ)),
        P(("dp", *SEQ), None),
        P(("dp", *SEQ)),
        P(("dp", *SEQ), None, None, "tensor"),
        P(None, "tensor", ("dp", *SEQ)),
        P(("dp", *SEQ), None, "tensor"),
        P("tensor", ("dp", *SEQ)),
    )
    out_specs = (
        P("dp", SEQ, None),
        P("dp", SEQ, None),
        P(("dp", *SEQ)),
        P(("dp", *SEQ), None, "tensor"),
        P(None, "tensor", ("dp", *SEQ)),
        P("tensor", ("dp", *SEQ)),
        P(("dp", *SEQ)),
        P(("dp", *SEQ), None),
        P(("dp", *SEQ)),
        P(("dp", *SEQ), None, None, "tensor"),
        P(None, "tensor", ("dp", *SEQ)),
        P(("dp", *SEQ), None, "tensor"),
        P("tensor", ("dp", *SEQ)),
    )
    fine = Mesh(mesh.devices.reshape(mesh.shape["dp"], 2, -1, 2), ("dp", *SEQ, "tensor"))
    return jax.shard_map(body, mesh=fine, in_specs=in_specs, out_specs=out_specs, check_vma=False)
```

```python
import functools
import math

import jax
import jax.numpy as jnp
from jax import lax
from jax.experimental import pallas as pl
from jax.experimental.pallas import tpu as pltpu
from jax.sharding import Mesh
from jax.sharding import PartitionSpec as P

HD = 128
TOPK = 4
PIC = 256

EPS = 1e-06
THETA = 1000000.0
MASKED = -1000000000.0

SEQ = ("z_hi", "ring")
GRID = ("z_hi", "ring", "tensor")
BF = jnp.bfloat16
F32 = jnp.float32
LANES = 128


def up_to(size, multiple):
    return -(-size // multiple) * multiple


def dot(a, b, dims):
    return lax.dot_general(a, b, (dims, ((), ())), preferred_element_type=F32)


def mm(a, b):
    return dot(a, b, ((1,), (0,)))


def mm_nt(a, b):
    return dot(a, b, ((1,), (1,)))


def mm_tn(a, b):
    return dot(a, b, ((0,), (0,)))


def rms_scale(values):
    return lax.rsqrt(jnp.mean(values * values, axis=-1, keepdims=True) + EPS)


def silu_grads(act_grad, gate_val, up_val):
    gate_sigmoid = jax.nn.sigmoid(gate_val)
    gate_grad = act_grad * up_val * gate_sigmoid * (1.0 + gate_val * (1.0 - gate_sigmoid))
    up_grad = act_grad * (gate_val * gate_sigmoid)
    return (gate_grad, up_grad)


def from_facing(x):
    flip = lax.axis_size("ring") * 2 + 1
    count = 2 * lax.axis_size("ring") * 2
    return lax.ppermute(x, GRID, [(i, i ^ flip) for i in range(count)])


def swap(x):
    return lax.ppermute(x, "tensor", [(0, 1), (1, 0)])


def together(*arrays):
    return lax.optimization_barrier(arrays)


UNITS = 384
EXPERTS = 8
SHARE_AT = 2
EXPERT_AT = 3
VMEM = 56 * 1024 * 1024


def feed_forward_kernel(
    capacity, expert_ref, h_ref, dy_ref, up_ref, down_ref, misc_ref,
    middle_ref, act_ref, dot_ref, prob_ref, scale_ref,
):
    part = pl.program_id(0)
    routed = part < pl.num_programs(0) - 1
    tokens, width = h_ref.shape
    expert = expert_ref[0]
    step = 256
    lane = lax.broadcasted_iota(jnp.int32, (step, LANES), 1)

    def column(x, at):
        return jnp.sum(jnp.where(lane == at, x, 0.0), axis=1, keepdims=True)

    @pl.when(part == 0)
    def _():
        for at in range(0, tokens, step):
            here = pl.ds(at, step)
            logits = mm(h_ref[here, :], misc_ref[...])
            among = (lane >= EXPERT_AT) & (lane < EXPERT_AT + EXPERTS)
            top = jnp.max(jnp.where(among, logits, -jnp.inf), axis=1, keepdims=True)
            raised = jnp.where(among, jnp.exp(jnp.where(among, logits - top, 0.0)), 0.0)
            probs = raised / jnp.sum(raised, axis=1, keepdims=True)
            share = jax.nn.sigmoid(column(logits, SHARE_AT))
            slot = column(dy_ref[here, width:].astype(F32), expert)
            gate = jnp.where(slot < capacity, column(probs, EXPERT_AT + expert), 0.0)
            prob_ref[here, :] = jnp.where(lane == SHARE_AT, share, probs)
            kept = jnp.where(slot < capacity, 1.0, 0.0)
            scale_ref[here, :] = jnp.where(
                lane == 0, gate, jnp.where(lane == 1, share, jnp.where(lane == 2, kept, 0.0))
            )
        dot_ref[...] = jnp.zeros_like(dot_ref)

    for at in range(0, tokens, step):
        here = pl.ds(at, step)
        gate_up = mm(h_ref[here, :], up_ref[...])
        back = mm(dy_ref[here, :width], down_ref[...])
        gate, up = gate_up[:, :UNITS], gate_up[:, UNITS:]
        scale = jnp.where(routed, scale_ref[here, 0:1], scale_ref[here, 1:2])
        counts = jnp.where(routed, scale_ref[here, 2:3], 1.0)
        sigma = jax.nn.sigmoid(gate)
        silu = gate * sigma
        act = (silu * up).astype(BF).astype(F32)
        dots = jnp.sum(act * back, axis=1, keepdims=True) * counts
        dot_ref[here, :] += jnp.where(lane == jnp.where(routed, expert, EXPERTS), dots, 0.0)
        back = back * scale
        act_ref[here, :] = (act * scale).astype(BF)
        middle_ref[here, :UNITS] = (back * up * sigma * (1.0 + gate * (1.0 - sigma))).astype(BF)
        middle_ref[here, UNITS:] = (back * silu).astype(BF)


def feed_forward(h, others, weights, misc, expert, capacity):
    tokens, width = h.shape
    parts = weights.shape[1] // (3 * UNITS)

    def whole(shape):
        return pl.BlockSpec(shape, lambda i, e: (0, 0), pipeline_mode=pl.Buffered(1))

    return pl.pallas_call(
        functools.partial(feed_forward_kernel, capacity),
        grid_spec=pltpu.PrefetchScalarGridSpec(
            num_scalar_prefetch=1,
            grid=(parts,),
            in_specs=[
                whole(h.shape),
                whole((tokens, width + LANES)),
                pl.BlockSpec((width, 2 * UNITS), lambda i, e: (0, i)),
                pl.BlockSpec((width, UNITS), lambda i, e: (0, 2 * parts + i)),
                whole(misc.shape),
            ],
            out_specs=[
                pl.BlockSpec((tokens, 2 * UNITS), lambda i, e: (0, i)),
                pl.BlockSpec((tokens, UNITS), lambda i, e: (0, i)),
                pl.BlockSpec((tokens, LANES), lambda i, e: (0, 0)),
                pl.BlockSpec((tokens, LANES), lambda i, e: (0, 0)),
            ],
            scratch_shapes=[pltpu.VMEM((tokens, LANES), F32)],
        ),
        out_shape=[
            jax.ShapeDtypeStruct((tokens, 2 * UNITS * parts), BF),
            jax.ShapeDtypeStruct((tokens, UNITS * parts), BF),
            jax.ShapeDtypeStruct((tokens, LANES), F32),
            jax.ShapeDtypeStruct((tokens, LANES), F32),
        ],
        compiler_params=pltpu.CompilerParams(vmem_limit_bytes=VMEM),
    )(expert, h, others, weights, weights, misc)


def ffn_rest_kernel(h_ref, dy_ref, middle_ref, act_ref, down_ref, grad_ref, out_ref):
    ups = middle_ref.shape[1]
    grad_ref[:, :ups] = mm_tn(h_ref[...], middle_ref[...]).astype(BF)
    grad_ref[:, ups:] = mm_tn(dy_ref[...], act_ref[...]).astype(BF)
    out_ref[...] = mm_nt(act_ref[...], down_ref[...]).astype(BF)


def ffn_rest(h, dy, middle, act, weights):
    tokens, width = h.shape
    ups, downs = middle.shape[1], act.shape[1]
    step = 256
    return pl.pallas_call(
        ffn_rest_kernel,
        grid=(width // step,),
        in_specs=[
            pl.BlockSpec((tokens, step), lambda i: (0, i)),
            pl.BlockSpec((tokens, step), lambda i: (0, i)),
            pl.BlockSpec((tokens, ups), lambda i: (0, 0)),
            pl.BlockSpec((tokens, downs), lambda i: (0, 0)),
            pl.BlockSpec((step, downs), lambda i: (i, ups // downs)),
        ],
        out_specs=[
            pl.BlockSpec((step, ups + downs), lambda i: (i, 0)),
            pl.BlockSpec((tokens, step), lambda i: (0, i)),
        ],
        out_shape=[
            jax.ShapeDtypeStruct((width, ups + downs), BF),
            jax.ShapeDtypeStruct((tokens, width), BF),
        ],
        compiler_params=pltpu.CompilerParams(vmem_limit_bytes=VMEM),
    )(h, dy, middle, act, weights)


def attn_grads_kernel(h_ref, linear_ref, small_ref, dx_ref, heads_ref, grad_ref):
    qkv = linear_ref.shape[1]
    grad_ref[:, :qkv] = mm_tn(h_ref[...], linear_ref[...]).astype(BF)
    grad_ref[:, qkv : qkv + LANES] = small_ref[...].T.astype(BF)
    grad_ref[:, qkv + LANES :] = mm_tn(dx_ref[...], heads_ref[...]).astype(BF)


def attn_grads(h, linear, small, dx, heads):
    tokens, width = h.shape
    rows, heads_width = heads.shape
    qkv = linear.shape[1]
    columns = qkv + LANES + heads_width
    step = 256
    return pl.pallas_call(
        attn_grads_kernel,
        grid=(width // step,),
        in_specs=[
            pl.BlockSpec((tokens, step), lambda i: (0, i)),
            pl.BlockSpec((tokens, qkv), lambda i: (0, 0)),
            pl.BlockSpec((LANES, step), lambda i: (0, i)),
            pl.BlockSpec((rows, step), lambda i: (0, i)),
            pl.BlockSpec((rows, heads_width), lambda i: (0, 0)),
        ],
        out_specs=pl.BlockSpec((step, columns), lambda i: (i, 0)),
        out_shape=jax.ShapeDtypeStruct((width, columns), BF),
        compiler_params=pltpu.CompilerParams(vmem_limit_bytes=VMEM),
    )(h, linear, small, dx, heads)


def plane_gather(x):
    n, width = x.shape
    count = lax.axis_size(SEQ) * lax.axis_size("tensor")
    copies = jnp.broadcast_to(x[None], (count, n, width))
    return lax.all_to_all(copies, GRID, 0, 0, tiled=True).reshape(count * n, width)


def send_parts(parts):
    count = lax.axis_size(SEQ) * lax.axis_size("tensor")
    parts = parts.astype(BF).reshape(count, -1, parts.shape[-1])
    return lax.all_to_all(parts, GRID, 0, 0, tiled=True)


def sum_parts(parts):
    return jnp.sum(parts.astype(F32), axis=0)


def plane_scatter(parts):
    return sum_parts(send_parts(parts))


def body(
    hidden_in,
    grad_out,
    expert_ids,
    slot_rank,
    piece_start,
    norm_attn,
    w_qkv,
    b_qkv,
    w_proj,
    norm_ffn,
    w_router,
    w_share_gate,
    expert_gate_up,
    expert_down,
    shared_gate_up,
    shared_down,
):
    seqs = lax.axis_size(SEQ)
    dps = lax.axis_size("dp")
    me_seq = lax.axis_index(SEQ)
    me_tensor = lax.axis_index("tensor")
    me = me_seq * 2 + me_tensor
    rows = hidden_in.shape[1]
    own = rows // 2
    length = rows * seqs
    depth = w_qkv.shape[0]
    width = depth * dps * seqs
    experts = expert_gate_up.shape[1]
    fe = expert_gate_up.shape[3]
    fs = shared_gate_up.shape[2] // seqs
    fe_pad = up_to(fe, UNITS)
    fs_pad = up_to(fs, UNITS)
    bias_part = b_qkv.shape[2]
    heads = b_qkv.shape[1]
    capacity = (5 * rows * TOPK + 4 * experts - 1) // (4 * experts)
    score_scale = 1.0 / math.sqrt(HD)

    def mine(x):
        return lax.dynamic_slice_in_dim(x, me_tensor * own, own, 0)

    def both_halves(x):
        other = swap(x)
        first = jnp.where(me_tensor == 0, x, other)
        second = jnp.where(me_tensor == 0, other, x)
        return jnp.concatenate([first, second], 0)

    flat_ids = expert_ids[0].reshape(-1)
    flat_rank = slot_rank[0].reshape(-1)
    earlier = (flat_rank[None, :] < flat_rank[:, None]) & (flat_ids[None, :] == flat_ids[:, None])
    position = jnp.sum(earlier.astype(jnp.int32), axis=1)
    position = jnp.where(position < capacity, position, LANES - 1)
    chosen = expert_ids[0][:, :, None] == jnp.arange(experts, dtype=jnp.int32)[None, None, :]
    slot_of = jnp.sum(
        jnp.where(chosen, position.reshape(rows, TOPK)[:, :, None] - (LANES - 1), 0), axis=1
    ) + (LANES - 1)
    slot_cols = jnp.pad(mine(slot_of).astype(BF), ((0, 0), (0, LANES - experts)))
    dy_own = mine(grad_out[0])
    x_own = mine(hidden_in[0])

    misc = jnp.concatenate(
        [norm_attn[:, None], norm_ffn[:, None], w_share_gate[:, None], w_router], axis=1
    )
    n_misc = misc.shape[1]
    bias_rows = b_qkv.transpose(1, 0, 2).reshape(heads, 3 * bias_part)
    bias_rows = jnp.pad(bias_rows, ((0, 0), (0, depth - 3 * bias_part)))
    attn_blob = jnp.concatenate(
        [
            w_qkv.reshape(depth, 3, heads, HD).transpose(2, 0, 1, 3).reshape(heads, depth, 3 * HD),
            jnp.broadcast_to(misc[None], (heads, depth, n_misc)),
            bias_rows[:, :, None],
            jnp.zeros((heads, depth, LANES - n_misc - 1), BF),
        ],
        axis=2,
    )
    def padded(x, units):
        return jnp.pad(x, ((0, 0), (0, 0), (0, units - x.shape[2])))

    units = fe_pad + fs_pad
    egu_blob = expert_gate_up.transpose(1, 2, 0, 3)
    sgu_blob = shared_gate_up.reshape(depth, 2, seqs, fs).transpose(2, 1, 0, 3)
    edn_blob = expert_down.transpose(0, 2, 1)
    sdn_blob = shared_down.reshape(seqs, fs, depth).transpose(0, 2, 1)
    columns = []
    for blob, blob_units in ((egu_blob, fe_pad), (sgu_blob, fs_pad)):
        gates, ups = padded(blob[:, 0], blob_units), padded(blob[:, 1], blob_units)
        for at in range(0, blob_units, UNITS):
            columns += [gates[:, :, at : at + UNITS], ups[:, :, at : at + UNITS]]
    columns += [padded(edn_blob, fe_pad), padded(sdn_blob, fs_pad)]
    ffn_blob = jnp.concatenate(columns, axis=2)

    first_ring = lax.axis_index("z_hi") == 0

    def both_rings(block):
        facing = from_facing(block)
        return jnp.stack(
            [jnp.where(first_ring, block, facing), jnp.where(first_ring, facing, block)]
        )

    x_all = lax.all_gather(both_rings(hidden_in[0]), "ring", axis=1, tiled=True)
    x_all = x_all.reshape(length, width)

    attn_blob = lax.all_to_all(attn_blob, SEQ, 0, 0, tiled=True).reshape(1, seqs * depth, -1)
    attn_full = jnp.broadcast_to(attn_blob, (dps, *attn_blob.shape[1:]))
    attn_full = lax.all_to_all(attn_full, "dp", 0, 0, tiled=True).reshape(width, -1)
    x_all, attn_full, proj_rows, ffn_blob = together(x_all, attn_full, w_proj.T, ffn_blob)
    proj_rows = lax.all_gather(proj_rows, ("dp", *SEQ), axis=0, tiled=True)
    qkv_full = attn_full[:, : 3 * HD]
    misc_full = attn_full[:, 3 * HD :]
    ffn_blob = lax.all_to_all(ffn_blob, SEQ, 0, 0, tiled=True)
    ffn_blob, dy_slots = together(ffn_blob, jnp.concatenate([dy_own, slot_cols], 1))
    dy_slots = plane_gather(dy_slots)

    bias_full = misc_full[:, n_misc].reshape(dps * seqs, depth)[:, : 3 * bias_part]
    bias_full = bias_full.reshape(dps * seqs, 3, bias_part).transpose(1, 0, 2).reshape(1, 3 * HD)
    misc_rows = misc_full[:, :n_misc].T.astype(F32)
    gain_attn = misc_rows[0:1]
    gain_ffn = misc_rows[1:2]

    positions = jnp.arange(length, dtype=jnp.int32)
    freq_table = jnp.exp(jnp.arange(HD // 2, dtype=F32) * (-2.0 * math.log(THETA) / HD))
    angle = positions.astype(F32)[:, None] * freq_table[None, :]
    cosine = jnp.cos(angle)
    sine = jnp.sin(angle)
    starts = piece_start[0]
    inside = (positions[:, None] >= starts[None, :]) & (
        positions[:, None] < starts[None, :] + PIC
    )
    labels = jnp.arange(starts.shape[0], dtype=jnp.int32)
    segment = jnp.max(jnp.where(inside, labels[None, :], -1), axis=1)

    def seen():
        causal = positions[None, :] <= positions[:, None]
        picture = (segment[:, None] == segment[None, :]) & (segment[:, None] >= 0)
        return causal | picture

    def rotate(values):
        lead, tail = values[:, : HD // 2], values[:, HD // 2 :]
        return jnp.concatenate([lead * cosine - tail * sine, tail * cosine + lead * sine], axis=1)

    def unrotate(values):
        lead, tail = values[:, : HD // 2], values[:, HD // 2 :]
        return jnp.concatenate([lead * cosine + tail * sine, tail * cosine - lead * sine], axis=1)

    resid_all = x_all.astype(F32)
    norm_one = resid_all * rms_scale(resid_all)
    normed_one = (norm_one * gain_attn).astype(BF)
    linear = mm(normed_one, qkv_full) + bias_full.astype(F32)
    query = rotate(linear[:, :HD]).astype(BF)
    key = rotate(linear[:, HD : 2 * HD]).astype(BF)
    value = linear[:, 2 * HD :].astype(BF)
    scores = jnp.where(seen(), mm_nt(query, key) * score_scale, MASKED)
    exp_scores = jnp.exp(scores - jnp.max(scores, axis=1, keepdims=True))
    attn_probs = exp_scores / jnp.sum(exp_scores, axis=1, keepdims=True)
    probs_low = attn_probs.astype(BF)
    attn_head = mm(probs_low, value).astype(BF)

    by_head, dy_slots = together(attn_head.reshape(seqs, rows, HD), dy_slots)
    by_head = lax.all_to_all(by_head, SEQ, 0, 0, tiled=True)
    by_head, ffn_blob = together(by_head, ffn_blob)
    ffn_full = lax.all_gather(ffn_blob.reshape(seqs * depth, -1), "dp", axis=0, tiled=True)
    w_up = ffn_full[:, : 2 * units]
    attn_flat = by_head.transpose(1, 0, 2).reshape(rows, heads * HD)
    attn_part = mm_nt(attn_flat, proj_rows)
    theirs = lax.dynamic_slice_in_dim(attn_part, (1 - me_tensor) * own, own, 0)
    attn_sum = mine(attn_part) + swap(theirs.astype(BF)).astype(F32)
    after_attn = x_own.astype(F32) + attn_sum
    scale_two = rms_scale(after_attn)
    norm_two = after_attn * scale_two
    normed_two = (norm_two * gain_ffn).astype(BF)
    h_all = plane_gather(normed_two)

    expert = me_seq.astype(jnp.int32).reshape(1)
    dgate_up, act_weighed, dots, router = feed_forward(
        h_all, dy_slots, ffn_full, misc_full, expert, capacity
    )
    back_parts = jnp.concatenate([mm_nt(dgate_up, w_up).astype(BF), dots.astype(BF)], 1)
    half = width // 2
    ffn_left = send_parts(mm_nt(act_weighed, ffn_full[:half, 2 * units :]))
    back_parts, act_weighed, dgate_up, ffn_left = together(
        back_parts, act_weighed, dgate_up, ffn_left
    )
    back = send_parts(back_parts)

    ffn_grad, ffn_parts = ffn_rest(h_all, dy_slots, dgate_up, act_weighed, ffn_full)
    back, ffn_parts, ffn_grad = together(back, ffn_parts, ffn_grad)
    back = sum_parts(back)
    ffn_grad = lax.psum_scatter(ffn_grad, "dp", scatter_dimension=0, tiled=True)

    router_own = lax.dynamic_slice_in_dim(router, me * own, own, 0)
    probs_own = router_own[:, EXPERT_AT : EXPERT_AT + experts]
    sig_own = router_own[:, SHARE_AT : SHARE_AT + 1]
    dprobs = back[:, width : width + experts]
    dlogits = probs_own * (dprobs - jnp.sum(probs_own * dprobs, axis=1, keepdims=True))
    dshare = back[:, width + experts : width + experts + 1] * sig_own * (1.0 - sig_own)
    dmisc = jnp.concatenate([jnp.zeros((own, 2), F32), dshare, dlogits], 1)
    dmisc = jnp.pad(dmisc, ((0, 0), (0, LANES - n_misc))).astype(BF)
    dh_two = back[:, :width] + mm_nt(dmisc, misc_full)
    grad_misc = mm_tn(dmisc, normed_two)
    grad_gain_ffn = jnp.sum(dh_two * norm_two, axis=0)
    inner_two = dh_two * gain_ffn
    dx_one = dy_own.astype(F32) + scale_two * (
        inner_two - norm_two * jnp.mean(inner_two * norm_two, axis=-1, keepdims=True)
    )
    dx_low = dx_one.astype(BF)

    dx_pair = both_halves(dx_low)
    do_flat = mm(dx_pair, proj_rows).astype(BF)
    do_heads = do_flat.reshape(rows, heads, HD).transpose(1, 0, 2)
    do_head = lax.all_to_all(do_heads, SEQ, 0, 0, tiled=True).reshape(length, HD)
    do_head, ffn_right = together(do_head, ffn_parts[:, half:])
    ffn_right = send_parts(ffn_right)
    dvalue = mm_tn(probs_low, do_head)
    dprob = mm_nt(do_head, value)
    row_delta = jnp.sum(attn_probs * dprob, axis=1, keepdims=True)
    dscore = (attn_probs * (dprob - row_delta)).astype(BF)
    dquery = mm(dscore, key) * score_scale
    dkey = mm_tn(dscore, query) * score_scale
    dlinear = jnp.concatenate([unrotate(dquery), unrotate(dkey), dvalue], 1).astype(BF)
    grad_bias = jnp.sum(dlinear.astype(F32), axis=0)
    dh_part = mm_nt(dlinear, qkv_full)
    grad_gain_attn = jnp.sum(dh_part * norm_one, axis=0)
    dh_low, ffn_right = together(dh_part.astype(BF), ffn_right)
    dh_sent = send_parts(dh_low)
    ffn_sum = jnp.concatenate([sum_parts(ffn_left), sum_parts(ffn_right)], 1)
    hidden_out = both_halves((after_attn + ffn_sum).astype(BF))

    bias_rows = grad_bias.reshape(3, dps * seqs, bias_part).transpose(1, 0, 2)
    bias_rows = bias_rows.reshape(dps * seqs, 3 * bias_part)
    bias_rows = jnp.pad(bias_rows, ((0, 0), (0, depth - 3 * bias_part))).reshape(1, width)
    small = jnp.concatenate(
        [grad_gain_attn[None], grad_gain_ffn[None], grad_misc[2:n_misc], bias_rows], 0
    )
    small = jnp.pad(small, ((0, LANES - n_misc - 1), (0, 0)))
    attn_grad = attn_grads(normed_one, dlinear, small, dx_pair, attn_flat)
    dh_sent, attn_grad, ffn_grad, hidden_out = together(
        dh_sent, attn_grad, ffn_grad, hidden_out
    )
    attn_grad = lax.psum_scatter(attn_grad, "dp", scatter_dimension=0, tiled=True)
    dh_one = sum_parts(dh_sent)
    resid = x_own.astype(F32)
    scale_one = rms_scale(resid)
    norm_own = resid * scale_one
    inner_one = dh_one * gain_attn
    grad_in = dx_one + scale_one * (
        inner_one - norm_own * jnp.mean(inner_one * norm_own, axis=-1, keepdims=True)
    )
    grad_in = both_halves(grad_in)
    ffn_grad = lax.all_to_all(ffn_grad.reshape(seqs, depth, -1), SEQ, 0, 0, tiled=True)
    ffn_grad, attn_grad, grad_in = together(ffn_grad, attn_grad, grad_in)
    attn_grad = attn_grad.reshape(seqs, depth, -1)
    attn_grad = lax.all_to_all(attn_grad, SEQ, 0, 0, tiled=True).astype(F32)

    def unit_columns(first, kind, size):
        at = [(2 * (first + i) + kind) * UNITS for i in range(up_to(size, UNITS) // UNITS)]
        picked = [
            ffn_grad[:, :, c : c + min(UNITS, size - i * UNITS)] for i, c in enumerate(at)
        ]
        return jnp.concatenate(picked, 2).astype(F32)

    shared_at = fe_pad // UNITS
    out_egu = jnp.stack([unit_columns(0, 0, fe), unit_columns(0, 1, fe)], 2).transpose(1, 0, 2, 3)
    out_sgu = [unit_columns(shared_at, kind, fs).transpose(1, 0, 2) for kind in (0, 1)]
    out_sgu = jnp.stack(out_sgu, 1).reshape(depth, 2, seqs * fs)
    down_at = 2 * units
    out_edn = ffn_grad[:, :, down_at : down_at + fe].transpose(0, 2, 1).astype(F32)
    out_sdn = ffn_grad[:, :, down_at + fe_pad : down_at + fe_pad + fs].transpose(0, 2, 1)
    out_sdn = out_sdn.reshape(seqs * fs, depth).astype(F32)
    out_qkv = attn_grad[:, :, : 3 * HD].reshape(heads, depth, 3, HD)
    out_qkv = out_qkv.transpose(1, 2, 0, 3).reshape(depth, 3, heads * HD)
    out_misc = jnp.sum(attn_grad[:, :, 3 * HD : 3 * HD + n_misc], axis=0)
    out_misc = out_misc + swap(out_misc)
    out_bias = attn_grad[:, : 3 * bias_part, 3 * HD + n_misc]
    out_bias = out_bias.reshape(heads, 3, bias_part).transpose(1, 0, 2)
    out_proj = jnp.sum(attn_grad[:, :, 3 * HD + LANES :], axis=0).T

    return (
        hidden_out[None],
        grad_in[None],
        out_misc[:, 0],
        out_qkv,
        out_bias,
        out_proj,
        out_misc[:, 1],
        out_misc[:, 3:n_misc],
        out_misc[:, 2],
        out_egu,
        out_edn,
        out_sgu,
        out_sdn,
    )


def solution(mesh):
    in_specs = (
        P("dp", SEQ, None),
        P("dp", SEQ, None),
        P("dp", SEQ, None),
        P("dp", SEQ, None),
        P("dp", None),
        P(("dp", *SEQ)),
        P(("dp", *SEQ), None, "tensor"),
        P(None, "tensor", ("dp", *SEQ)),
        P("tensor", ("dp", *SEQ)),
        P(("dp", *SEQ)),
        P(("dp", *SEQ), None),
        P(("dp", *SEQ)),
        P(("dp", *SEQ), None, None, "tensor"),
        P(None, "tensor", ("dp", *SEQ)),
        P(("dp", *SEQ), None, "tensor"),
        P("tensor", ("dp", *SEQ)),
    )
    out_specs = (
        P("dp", SEQ, None),
        P("dp", SEQ, None),
        P(("dp", *SEQ)),
        P(("dp", *SEQ), None, "tensor"),
        P(None, "tensor", ("dp", *SEQ)),
        P("tensor", ("dp", *SEQ)),
        P(("dp", *SEQ)),
        P(("dp", *SEQ), None),
        P(("dp", *SEQ)),
        P(("dp", *SEQ), None, None, "tensor"),
        P(None, "tensor", ("dp", *SEQ)),
        P(("dp", *SEQ), None, "tensor"),
        P("tensor", ("dp", *SEQ)),
    )
    fine = Mesh(mesh.devices.reshape(mesh.shape["dp"], 2, -1, 2), ("dp", *SEQ, "tensor"))
    return jax.shard_map(body, mesh=fine, in_specs=in_specs, out_specs=out_specs, check_vma=False)
```

```python
import functools
import math

import jax
import jax.numpy as jnp
from jax import lax
from jax.experimental import pallas as pl
from jax.experimental.pallas import tpu as pltpu
from jax.sharding import Mesh
from jax.sharding import PartitionSpec as P

HD = 128
TOPK = 4
PIC = 256

EPS = 1e-06
THETA = 1000000.0
MASKED = -1000000000.0

SEQ = ("z_hi", "ring")
GRID = ("z_hi", "ring", "tensor")
BF = jnp.bfloat16
F32 = jnp.float32
LANES = 128


def up_to(size, multiple):
    return -(-size // multiple) * multiple


def dot(a, b, dims):
    return lax.dot_general(a, b, (dims, ((), ())), preferred_element_type=F32)


def mm(a, b):
    return dot(a, b, ((1,), (0,)))


def mm_nt(a, b):
    return dot(a, b, ((1,), (1,)))


def mm_tn(a, b):
    return dot(a, b, ((0,), (0,)))


def rms_scale(values):
    return lax.rsqrt(jnp.mean(values * values, axis=-1, keepdims=True) + EPS)


def silu_grads(act_grad, gate_val, up_val):
    gate_sigmoid = jax.nn.sigmoid(gate_val)
    gate_grad = act_grad * up_val * gate_sigmoid * (1.0 + gate_val * (1.0 - gate_sigmoid))
    up_grad = act_grad * (gate_val * gate_sigmoid)
    return (gate_grad, up_grad)


def from_facing(x):
    flip = lax.axis_size("ring") * 2 + 1
    count = 2 * lax.axis_size("ring") * 2
    return lax.ppermute(x, GRID, [(i, i ^ flip) for i in range(count)])


def swap(x):
    return lax.ppermute(x, "tensor", [(0, 1), (1, 0)])


def together(*arrays):
    return lax.optimization_barrier(arrays)


UNITS = 384
EXPERTS = 8
SHARE_AT = 2
EXPERT_AT = 3
VMEM = 56 * 1024 * 1024


def feed_forward_kernel(
    capacity, expert_ref, h_ref, dy_ref, up_ref, down_ref, misc_ref,
    middle_ref, act_ref, dot_ref, prob_ref, scale_ref,
):
    part = pl.program_id(0)
    routed = part < pl.num_programs(0) - 1
    tokens, width = h_ref.shape
    expert = expert_ref[0]
    step = 256
    lane = lax.broadcasted_iota(jnp.int32, (step, LANES), 1)

    def column(x, at):
        return jnp.sum(jnp.where(lane == at, x, 0.0), axis=1, keepdims=True)

    @pl.when(part == 0)
    def _():
        for at in range(0, tokens, step):
            here = pl.ds(at, step)
            logits = mm(h_ref[here, :], misc_ref[...])
            among = (lane >= EXPERT_AT) & (lane < EXPERT_AT + EXPERTS)
            top = jnp.max(jnp.where(among, logits, -jnp.inf), axis=1, keepdims=True)
            raised = jnp.where(among, jnp.exp(jnp.where(among, logits - top, 0.0)), 0.0)
            probs = raised / jnp.sum(raised, axis=1, keepdims=True)
            share = jax.nn.sigmoid(column(logits, SHARE_AT))
            slot = column(dy_ref[here, width:].astype(F32), expert)
            gate = jnp.where(slot < capacity, column(probs, EXPERT_AT + expert), 0.0)
            prob_ref[here, :] = jnp.where(lane == SHARE_AT, share, probs)
            kept = jnp.where(slot < capacity, 1.0, 0.0)
            scale_ref[here, :] = jnp.where(
                lane == 0, gate, jnp.where(lane == 1, share, jnp.where(lane == 2, kept, 0.0))
            )
        dot_ref[...] = jnp.zeros_like(dot_ref)

    for at in range(0, tokens, step):
        here = pl.ds(at, step)
        gate_up = mm(h_ref[here, :], up_ref[...])
        back = mm(dy_ref[here, :width], down_ref[...])
        gate, up = gate_up[:, :UNITS], gate_up[:, UNITS:]
        scale = jnp.where(routed, scale_ref[here, 0:1], scale_ref[here, 1:2])
        counts = jnp.where(routed, scale_ref[here, 2:3], 1.0)
        sigma = jax.nn.sigmoid(gate)
        silu = gate * sigma
        act = (silu * up).astype(BF).astype(F32)
        dots = jnp.sum(act * back, axis=1, keepdims=True) * counts
        dot_ref[here, :] += jnp.where(lane == jnp.where(routed, expert, EXPERTS), dots, 0.0)
        back = back * scale
        act_ref[here, :] = (act * scale).astype(BF)
        middle_ref[here, :UNITS] = (back * up * sigma * (1.0 + gate * (1.0 - sigma))).astype(BF)
        middle_ref[here, UNITS:] = (back * silu).astype(BF)


def feed_forward(h, others, weights, misc, expert, capacity):
    tokens, width = h.shape
    parts = weights.shape[1] // (3 * UNITS)

    def whole(shape):
        return pl.BlockSpec(shape, lambda i, e: (0, 0), pipeline_mode=pl.Buffered(1))

    return pl.pallas_call(
        functools.partial(feed_forward_kernel, capacity),
        grid_spec=pltpu.PrefetchScalarGridSpec(
            num_scalar_prefetch=1,
            grid=(parts,),
            in_specs=[
                whole(h.shape),
                whole((tokens, width + LANES)),
                pl.BlockSpec((width, 2 * UNITS), lambda i, e: (0, i)),
                pl.BlockSpec((width, UNITS), lambda i, e: (0, 2 * parts + i)),
                whole(misc.shape),
            ],
            out_specs=[
                pl.BlockSpec((tokens, 2 * UNITS), lambda i, e: (0, i)),
                pl.BlockSpec((tokens, UNITS), lambda i, e: (0, i)),
                pl.BlockSpec((tokens, LANES), lambda i, e: (0, 0)),
                pl.BlockSpec((tokens, LANES), lambda i, e: (0, 0)),
            ],
            scratch_shapes=[pltpu.VMEM((tokens, LANES), F32)],
        ),
        out_shape=[
            jax.ShapeDtypeStruct((tokens, 2 * UNITS * parts), BF),
            jax.ShapeDtypeStruct((tokens, UNITS * parts), BF),
            jax.ShapeDtypeStruct((tokens, LANES), F32),
            jax.ShapeDtypeStruct((tokens, LANES), F32),
        ],
        compiler_params=pltpu.CompilerParams(vmem_limit_bytes=VMEM),
    )(expert, h, others, weights, weights, misc)


def ffn_rest_kernel(h_ref, dy_ref, middle_ref, act_ref, down_ref, grad_ref, out_ref):
    ups = middle_ref.shape[1]
    grad_ref[:, :ups] = mm_tn(h_ref[...], middle_ref[...]).astype(BF)
    grad_ref[:, ups:] = mm_tn(dy_ref[...], act_ref[...]).astype(BF)
    out_ref[...] = mm_nt(act_ref[...], down_ref[...]).astype(BF)


def ffn_rest(h, dy, middle, act, weights):
    tokens, width = h.shape
    ups, downs = middle.shape[1], act.shape[1]
    step = 256
    return pl.pallas_call(
        ffn_rest_kernel,
        grid=(width // step,),
        in_specs=[
            pl.BlockSpec((tokens, step), lambda i: (0, i)),
            pl.BlockSpec((tokens, step), lambda i: (0, i)),
            pl.BlockSpec((tokens, ups), lambda i: (0, 0)),
            pl.BlockSpec((tokens, downs), lambda i: (0, 0)),
            pl.BlockSpec((step, downs), lambda i: (i, ups // downs)),
        ],
        out_specs=[
            pl.BlockSpec((step, ups + downs), lambda i: (i, 0)),
            pl.BlockSpec((tokens, step), lambda i: (0, i)),
        ],
        out_shape=[
            jax.ShapeDtypeStruct((width, ups + downs), BF),
            jax.ShapeDtypeStruct((tokens, width), BF),
        ],
        compiler_params=pltpu.CompilerParams(vmem_limit_bytes=VMEM),
    )(h, dy, middle, act, weights)


def attn_grads_kernel(h_ref, linear_ref, small_ref, dx_ref, heads_ref, grad_ref):
    qkv = linear_ref.shape[1]
    grad_ref[:, :qkv] = mm_tn(h_ref[...], linear_ref[...]).astype(BF)
    grad_ref[:, qkv : qkv + LANES] = small_ref[...].T.astype(BF)
    grad_ref[:, qkv + LANES :] = mm_tn(dx_ref[...], heads_ref[...]).astype(BF)


def attn_grads(h, linear, small, dx, heads):
    tokens, width = h.shape
    rows, heads_width = heads.shape
    qkv = linear.shape[1]
    columns = qkv + LANES + heads_width
    step = 256
    return pl.pallas_call(
        attn_grads_kernel,
        grid=(width // step,),
        in_specs=[
            pl.BlockSpec((tokens, step), lambda i: (0, i)),
            pl.BlockSpec((tokens, qkv), lambda i: (0, 0)),
            pl.BlockSpec((LANES, step), lambda i: (0, i)),
            pl.BlockSpec((rows, step), lambda i: (0, i)),
            pl.BlockSpec((rows, heads_width), lambda i: (0, 0)),
        ],
        out_specs=pl.BlockSpec((step, columns), lambda i: (i, 0)),
        out_shape=jax.ShapeDtypeStruct((width, columns), BF),
        compiler_params=pltpu.CompilerParams(vmem_limit_bytes=VMEM),
    )(h, linear, small, dx, heads)


def plane_gather(x):
    n, width = x.shape
    count = lax.axis_size(SEQ) * lax.axis_size("tensor")
    copies = jnp.broadcast_to(x[None], (count, n, width))
    return lax.all_to_all(copies, GRID, 0, 0, tiled=True).reshape(count * n, width)


def send_parts(parts):
    count = lax.axis_size(SEQ) * lax.axis_size("tensor")
    parts = parts.astype(BF).reshape(count, -1, parts.shape[-1])
    return lax.all_to_all(parts, GRID, 0, 0, tiled=True)


def sum_parts(parts):
    return jnp.sum(parts.astype(F32), axis=0)


def plane_scatter(parts):
    return sum_parts(send_parts(parts))


def body(
    hidden_in,
    grad_out,
    expert_ids,
    slot_rank,
    piece_start,
    norm_attn,
    w_qkv,
    b_qkv,
    w_proj,
    norm_ffn,
    w_router,
    w_share_gate,
    expert_gate_up,
    expert_down,
    shared_gate_up,
    shared_down,
):
    seqs = lax.axis_size(SEQ)
    dps = lax.axis_size("dp")
    me_seq = lax.axis_index(SEQ)
    me_tensor = lax.axis_index("tensor")
    me = me_seq * 2 + me_tensor
    rows = hidden_in.shape[1]
    own = rows // 2
    length = rows * seqs
    depth = w_qkv.shape[0]
    width = depth * dps * seqs
    experts = expert_gate_up.shape[1]
    fe = expert_gate_up.shape[3]
    fs = shared_gate_up.shape[2] // seqs
    fe_pad = up_to(fe, UNITS)
    fs_pad = up_to(fs, UNITS)
    bias_part = b_qkv.shape[2]
    heads = b_qkv.shape[1]
    capacity = (5 * rows * TOPK + 4 * experts - 1) // (4 * experts)
    score_scale = 1.0 / math.sqrt(HD)

    def mine(x):
        return lax.dynamic_slice_in_dim(x, me_tensor * own, own, 0)

    def both_halves(x):
        other = swap(x)
        first = jnp.where(me_tensor == 0, x, other)
        second = jnp.where(me_tensor == 0, other, x)
        return jnp.concatenate([first, second], 0)

    flat_ids = expert_ids[0].reshape(-1)
    flat_rank = slot_rank[0].reshape(-1)
    earlier = (flat_rank[None, :] < flat_rank[:, None]) & (flat_ids[None, :] == flat_ids[:, None])
    position = jnp.sum(earlier.astype(jnp.int32), axis=1)
    position = jnp.where(position < capacity, position, LANES - 1)
    chosen = expert_ids[0][:, :, None] == jnp.arange(experts, dtype=jnp.int32)[None, None, :]
    slot_of = jnp.sum(
        jnp.where(chosen, position.reshape(rows, TOPK)[:, :, None] - (LANES - 1), 0), axis=1
    ) + (LANES - 1)
    slot_cols = jnp.pad(mine(slot_of).astype(BF), ((0, 0), (0, LANES - experts)))
    dy_own = mine(grad_out[0])
    x_own = mine(hidden_in[0])

    misc = jnp.concatenate(
        [norm_attn[:, None], norm_ffn[:, None], w_share_gate[:, None], w_router], axis=1
    )
    n_misc = misc.shape[1]
    bias_rows = b_qkv.transpose(1, 0, 2).reshape(heads, 3 * bias_part)
    bias_rows = jnp.pad(bias_rows, ((0, 0), (0, depth - 3 * bias_part)))
    attn_blob = jnp.concatenate(
        [
            w_qkv.reshape(depth, 3, heads, HD).transpose(2, 0, 1, 3).reshape(heads, depth, 3 * HD),
            jnp.broadcast_to(misc[None], (heads, depth, n_misc)),
            bias_rows[:, :, None],
            jnp.zeros((heads, depth, LANES - n_misc - 1), BF),
            jnp.broadcast_to(w_proj.T[None], (heads, depth, heads * HD)),
        ],
        axis=2,
    )
    def padded(x, units):
        return jnp.pad(x, ((0, 0), (0, 0), (0, units - x.shape[2])))

    units = fe_pad + fs_pad
    egu_blob = expert_gate_up.transpose(1, 2, 0, 3)
    sgu_blob = shared_gate_up.reshape(depth, 2, seqs, fs).transpose(2, 1, 0, 3)
    edn_blob = expert_down.transpose(0, 2, 1)
    sdn_blob = shared_down.reshape(seqs, fs, depth).transpose(0, 2, 1)
    columns = []
    for blob, blob_units in ((egu_blob, fe_pad), (sgu_blob, fs_pad)):
        gates, ups = padded(blob[:, 0], blob_units), padded(blob[:, 1], blob_units)
        for at in range(0, blob_units, UNITS):
            columns += [gates[:, :, at : at + UNITS], ups[:, :, at : at + UNITS]]
    columns += [padded(edn_blob, fe_pad), padded(sdn_blob, fs_pad)]
    ffn_blob = jnp.concatenate(columns, axis=2)

    first_ring = lax.axis_index("z_hi") == 0

    def both_rings(block):
        facing = from_facing(block)
        return jnp.stack(
            [jnp.where(first_ring, block, facing), jnp.where(first_ring, facing, block)]
        )

    x_all = lax.all_gather(both_rings(hidden_in[0]), "ring", axis=1, tiled=True)
    x_all = x_all.reshape(length, width)

    attn_blob = lax.all_to_all(attn_blob, SEQ, 0, 0, tiled=True).reshape(seqs * depth, -1)
    attn_cols = 3 * HD + LANES
    proj_rows = attn_blob[:, attn_cols:]
    attn_full = jnp.broadcast_to(attn_blob[None, :, :attn_cols], (dps, seqs * depth, attn_cols))
    attn_full = lax.all_to_all(attn_full, "dp", 0, 0, tiled=True).reshape(width, -1)
    x_all, attn_full, proj_rows, ffn_blob = together(x_all, attn_full, proj_rows, ffn_blob)
    proj_rows = lax.all_gather(proj_rows, "dp", axis=0, tiled=True)
    qkv_full = attn_full[:, : 3 * HD]
    misc_full = attn_full[:, 3 * HD :]
    ffn_blob = lax.all_to_all(ffn_blob, SEQ, 0, 0, tiled=True)

    bias_full = misc_full[:, n_misc].reshape(dps * seqs, depth)[:, : 3 * bias_part]
    bias_full = bias_full.reshape(dps * seqs, 3, bias_part).transpose(1, 0, 2).reshape(1, 3 * HD)
    misc_rows = misc_full[:, :n_misc].T.astype(F32)
    gain_attn = misc_rows[0:1]
    gain_ffn = misc_rows[1:2]

    positions = jnp.arange(length, dtype=jnp.int32)
    freq_table = jnp.exp(jnp.arange(HD // 2, dtype=F32) * (-2.0 * math.log(THETA) / HD))
    angle = positions.astype(F32)[:, None] * freq_table[None, :]
    cosine = jnp.cos(angle)
    sine = jnp.sin(angle)
    starts = piece_start[0]
    inside = (positions[:, None] >= starts[None, :]) & (
        positions[:, None] < starts[None, :] + PIC
    )
    labels = jnp.arange(starts.shape[0], dtype=jnp.int32)
    segment = jnp.max(jnp.where(inside, labels[None, :], -1), axis=1)

    def seen():
        causal = positions[None, :] <= positions[:, None]
        picture = (segment[:, None] == segment[None, :]) & (segment[:, None] >= 0)
        return causal | picture

    def rotate(values):
        lead, tail = values[:, : HD // 2], values[:, HD // 2 :]
        return jnp.concatenate([lead * cosine - tail * sine, tail * cosine + lead * sine], axis=1)

    def unrotate(values):
        lead, tail = values[:, : HD // 2], values[:, HD // 2 :]
        return jnp.concatenate([lead * cosine + tail * sine, tail * cosine - lead * sine], axis=1)

    resid_all = x_all.astype(F32)
    norm_one = resid_all * rms_scale(resid_all)
    normed_one = (norm_one * gain_attn).astype(BF)
    linear = mm(normed_one, qkv_full) + bias_full.astype(F32)
    query = rotate(linear[:, :HD]).astype(BF)
    key = rotate(linear[:, HD : 2 * HD]).astype(BF)
    value = linear[:, 2 * HD :].astype(BF)
    scores = jnp.where(seen(), mm_nt(query, key) * score_scale, MASKED)
    exp_scores = jnp.exp(scores - jnp.max(scores, axis=1, keepdims=True))
    attn_probs = exp_scores / jnp.sum(exp_scores, axis=1, keepdims=True)
    probs_low = attn_probs.astype(BF)
    attn_head = mm(probs_low, value).astype(BF)

    by_head, ffn_blob = together(attn_head.reshape(seqs, rows, HD), ffn_blob)
    by_head = lax.all_to_all(by_head, SEQ, 0, 0, tiled=True)
    dy_slots = jnp.concatenate([dy_own, slot_cols], 1)
    by_head, ffn_blob, dy_slots = together(by_head, ffn_blob, dy_slots)
    dy_slots = plane_gather(dy_slots)
    ffn_full = lax.all_gather(ffn_blob.reshape(seqs * depth, -1), "dp", axis=0, tiled=True)
    w_up = ffn_full[:, : 2 * units]
    attn_flat = by_head.transpose(1, 0, 2).reshape(rows, heads * HD)
    attn_part = mm_nt(attn_flat, proj_rows)
    theirs = lax.dynamic_slice_in_dim(attn_part, (1 - me_tensor) * own, own, 0)
    attn_sum = mine(attn_part) + swap(theirs.astype(BF)).astype(F32)
    after_attn = x_own.astype(F32) + attn_sum
    scale_two = rms_scale(after_attn)
    norm_two = after_attn * scale_two
    normed_two = (norm_two * gain_ffn).astype(BF)
    normed_sent, dy_slots = together(normed_two, dy_slots)
    h_all = plane_gather(normed_sent)

    expert = me_seq.astype(jnp.int32).reshape(1)
    dgate_up, act_weighed, dots, router = feed_forward(
        h_all, dy_slots, ffn_full, misc_full, expert, capacity
    )
    back_parts = jnp.concatenate([mm_nt(dgate_up, w_up).astype(BF), dots.astype(BF)], 1)
    half = width // 2
    ffn_left = send_parts(mm_nt(act_weighed, ffn_full[:half, 2 * units :]))
    back_parts, act_weighed, dgate_up, ffn_left = together(
        back_parts, act_weighed, dgate_up, ffn_left
    )
    back = send_parts(back_parts)

    ffn_grad, ffn_parts = ffn_rest(h_all, dy_slots, dgate_up, act_weighed, ffn_full)
    back, ffn_parts, ffn_grad = together(back, ffn_parts, ffn_grad)
    back = sum_parts(back)
    ffn_grad = lax.psum_scatter(ffn_grad, "dp", scatter_dimension=0, tiled=True)

    router_own = lax.dynamic_slice_in_dim(router, me * own, own, 0)
    probs_own = router_own[:, EXPERT_AT : EXPERT_AT + experts]
    sig_own = router_own[:, SHARE_AT : SHARE_AT + 1]
    dprobs = back[:, width : width + experts]
    dlogits = probs_own * (dprobs - jnp.sum(probs_own * dprobs, axis=1, keepdims=True))
    dshare = back[:, width + experts : width + experts + 1] * sig_own * (1.0 - sig_own)
    dmisc = jnp.concatenate([jnp.zeros((own, 2), F32), dshare, dlogits], 1)
    dmisc = jnp.pad(dmisc, ((0, 0), (0, LANES - n_misc))).astype(BF)
    dh_two = back[:, :width] + mm_nt(dmisc, misc_full)
    grad_misc = mm_tn(dmisc, normed_two)
    grad_gain_ffn = jnp.sum(dh_two * norm_two, axis=0)
    inner_two = dh_two * gain_ffn
    dx_one = dy_own.astype(F32) + scale_two * (
        inner_two - norm_two * jnp.mean(inner_two * norm_two, axis=-1, keepdims=True)
    )
    dx_low = dx_one.astype(BF)

    dx_pair = both_halves(dx_low)
    do_flat = mm(dx_pair, proj_rows).astype(BF)
    do_heads = do_flat.reshape(rows, heads, HD).transpose(1, 0, 2)
    do_head = lax.all_to_all(do_heads, SEQ, 0, 0, tiled=True).reshape(length, HD)
    do_head, ffn_right = together(do_head, ffn_parts[:, half:])
    ffn_right = send_parts(ffn_right)
    dvalue = mm_tn(probs_low, do_head)
    dprob = mm_nt(do_head, value)
    row_delta = jnp.sum(attn_probs * dprob, axis=1, keepdims=True)
    dscore = (attn_probs * (dprob - row_delta)).astype(BF)
    dquery = mm(dscore, key) * score_scale
    dkey = mm_tn(dscore, query) * score_scale
    dlinear = jnp.concatenate([unrotate(dquery), unrotate(dkey), dvalue], 1).astype(BF)
    grad_bias = jnp.sum(dlinear.astype(F32), axis=0)
    dh_part = mm_nt(dlinear, qkv_full)
    grad_gain_attn = jnp.sum(dh_part * norm_one, axis=0)
    dh_low, ffn_right = together(dh_part.astype(BF), ffn_right)
    dh_sent = send_parts(dh_low)
    ffn_sum = jnp.concatenate([sum_parts(ffn_left), sum_parts(ffn_right)], 1)
    hidden_out = both_halves((after_attn + ffn_sum).astype(BF))

    bias_rows = grad_bias.reshape(3, dps * seqs, bias_part).transpose(1, 0, 2)
    bias_rows = bias_rows.reshape(dps * seqs, 3 * bias_part)
    bias_rows = jnp.pad(bias_rows, ((0, 0), (0, depth - 3 * bias_part))).reshape(1, width)
    small = jnp.concatenate(
        [grad_gain_attn[None], grad_gain_ffn[None], grad_misc[2:n_misc], bias_rows], 0
    )
    small = jnp.pad(small, ((0, LANES - n_misc - 1), (0, 0)))
    attn_grad = attn_grads(normed_one, dlinear, small, dx_pair, attn_flat)
    dh_sent, attn_grad, ffn_grad, hidden_out = together(
        dh_sent, attn_grad, ffn_grad, hidden_out
    )
    attn_grad = lax.psum_scatter(attn_grad, "dp", scatter_dimension=0, tiled=True)
    dh_one = sum_parts(dh_sent)
    resid = x_own.astype(F32)
    scale_one = rms_scale(resid)
    norm_own = resid * scale_one
    inner_one = dh_one * gain_attn
    grad_in = dx_one + scale_one * (
        inner_one - norm_own * jnp.mean(inner_one * norm_own, axis=-1, keepdims=True)
    )
    grad_in = both_halves(grad_in)
    ffn_grad = lax.all_to_all(ffn_grad.reshape(seqs, depth, -1), SEQ, 0, 0, tiled=True)
    ffn_grad, attn_grad, grad_in = together(ffn_grad, attn_grad, grad_in)
    attn_grad = attn_grad.reshape(seqs, depth, -1)
    attn_grad = lax.all_to_all(attn_grad, SEQ, 0, 0, tiled=True).astype(F32)

    def unit_columns(first, kind, size):
        at = [(2 * (first + i) + kind) * UNITS for i in range(up_to(size, UNITS) // UNITS)]
        picked = [
            ffn_grad[:, :, c : c + min(UNITS, size - i * UNITS)] for i, c in enumerate(at)
        ]
        return jnp.concatenate(picked, 2).astype(F32)

    shared_at = fe_pad // UNITS
    out_egu = jnp.stack([unit_columns(0, 0, fe), unit_columns(0, 1, fe)], 2).transpose(1, 0, 2, 3)
    out_sgu = [unit_columns(shared_at, kind, fs).transpose(1, 0, 2) for kind in (0, 1)]
    out_sgu = jnp.stack(out_sgu, 1).reshape(depth, 2, seqs * fs)
    down_at = 2 * units
    out_edn = ffn_grad[:, :, down_at : down_at + fe].transpose(0, 2, 1).astype(F32)
    out_sdn = ffn_grad[:, :, down_at + fe_pad : down_at + fe_pad + fs].transpose(0, 2, 1)
    out_sdn = out_sdn.reshape(seqs * fs, depth).astype(F32)
    out_qkv = attn_grad[:, :, : 3 * HD].reshape(heads, depth, 3, HD)
    out_qkv = out_qkv.transpose(1, 2, 0, 3).reshape(depth, 3, heads * HD)
    out_misc = jnp.sum(attn_grad[:, :, 3 * HD : 3 * HD + n_misc], axis=0)
    out_misc = out_misc + swap(out_misc)
    out_bias = attn_grad[:, : 3 * bias_part, 3 * HD + n_misc]
    out_bias = out_bias.reshape(heads, 3, bias_part).transpose(1, 0, 2)
    out_proj = jnp.sum(attn_grad[:, :, 3 * HD + LANES :], axis=0).T

    return (
        hidden_out[None],
        grad_in[None],
        out_misc[:, 0],
        out_qkv,
        out_bias,
        out_proj,
        out_misc[:, 1],
        out_misc[:, 3:n_misc],
        out_misc[:, 2],
        out_egu,
        out_edn,
        out_sgu,
        out_sdn,
    )


def solution(mesh):
    in_specs = (
        P("dp", SEQ, None),
        P("dp", SEQ, None),
        P("dp", SEQ, None),
        P("dp", SEQ, None),
        P("dp", None),
        P(("dp", *SEQ)),
        P(("dp", *SEQ), None, "tensor"),
        P(None, "tensor", ("dp", *SEQ)),
        P("tensor", ("dp", *SEQ)),
        P(("dp", *SEQ)),
        P(("dp", *SEQ), None),
        P(("dp", *SEQ)),
        P(("dp", *SEQ), None, None, "tensor"),
        P(None, "tensor", ("dp", *SEQ)),
        P(("dp", *SEQ), None, "tensor"),
        P("tensor", ("dp", *SEQ)),
    )
    out_specs = (
        P("dp", SEQ, None),
        P("dp", SEQ, None),
        P(("dp", *SEQ)),
        P(("dp", *SEQ), None, "tensor"),
        P(None, "tensor", ("dp", *SEQ)),
        P("tensor", ("dp", *SEQ)),
        P(("dp", *SEQ)),
        P(("dp", *SEQ), None),
        P(("dp", *SEQ)),
        P(("dp", *SEQ), None, None, "tensor"),
        P(None, "tensor", ("dp", *SEQ)),
        P(("dp", *SEQ), None, "tensor"),
        P("tensor", ("dp", *SEQ)),
    )
    fine = Mesh(mesh.devices.reshape(mesh.shape["dp"], 2, -1, 2), ("dp", *SEQ, "tensor"))
    return jax.shard_map(body, mesh=fine, in_specs=in_specs, out_specs=out_specs, check_vma=False)
```

```python
import functools
import math

import jax
import jax.numpy as jnp
from jax import lax
from jax.experimental import pallas as pl
from jax.experimental.pallas import tpu as pltpu
from jax.sharding import Mesh
from jax.sharding import PartitionSpec as P

HD = 128
TOPK = 4
PIC = 256

EPS = 1e-06
THETA = 1000000.0
MASKED = -1000000000.0

SEQ = ("z_hi", "ring")
GRID = ("z_hi", "ring", "tensor")
BF = jnp.bfloat16
F32 = jnp.float32
LANES = 128


def up_to(size, multiple):
    return -(-size // multiple) * multiple


def dot(a, b, dims):
    return lax.dot_general(a, b, (dims, ((), ())), preferred_element_type=F32)


def mm(a, b):
    return dot(a, b, ((1,), (0,)))


def mm_nt(a, b):
    return dot(a, b, ((1,), (1,)))


def mm_tn(a, b):
    return dot(a, b, ((0,), (0,)))


def rms_scale(values):
    return lax.rsqrt(jnp.mean(values * values, axis=-1, keepdims=True) + EPS)


def silu_grads(act_grad, gate_val, up_val):
    gate_sigmoid = jax.nn.sigmoid(gate_val)
    gate_grad = act_grad * up_val * gate_sigmoid * (1.0 + gate_val * (1.0 - gate_sigmoid))
    up_grad = act_grad * (gate_val * gate_sigmoid)
    return (gate_grad, up_grad)


def from_facing(x):
    flip = lax.axis_size("ring") * 2 + 1
    count = 2 * lax.axis_size("ring") * 2
    return lax.ppermute(x, GRID, [(i, i ^ flip) for i in range(count)])


def swap(x):
    return lax.ppermute(x, "tensor", [(0, 1), (1, 0)])


def together(*arrays):
    return lax.optimization_barrier(arrays)


UNITS = 384
EXPERTS = 8
SHARE_AT = 2
EXPERT_AT = 3
VMEM = 56 * 1024 * 1024


def feed_forward_kernel(
    capacity, expert_ref, h_ref, dy_ref, up_ref, down_ref, misc_ref,
    middle_ref, act_ref, dot_ref, prob_ref, scale_ref,
):
    part = pl.program_id(0)
    routed = part < pl.num_programs(0) - 1
    tokens, width = h_ref.shape
    expert = expert_ref[0]
    step = 256
    lane = lax.broadcasted_iota(jnp.int32, (step, LANES), 1)

    def column(x, at):
        return jnp.sum(jnp.where(lane == at, x, 0.0), axis=1, keepdims=True)

    @pl.when(part == 0)
    def _():
        for at in range(0, tokens, step):
            here = pl.ds(at, step)
            logits = mm(h_ref[here, :], misc_ref[...])
            among = (lane >= EXPERT_AT) & (lane < EXPERT_AT + EXPERTS)
            top = jnp.max(jnp.where(among, logits, -jnp.inf), axis=1, keepdims=True)
            raised = jnp.where(among, jnp.exp(jnp.where(among, logits - top, 0.0)), 0.0)
            probs = raised / jnp.sum(raised, axis=1, keepdims=True)
            share = jax.nn.sigmoid(column(logits, SHARE_AT))
            slot = column(dy_ref[here, width:].astype(F32), expert)
            gate = jnp.where(slot < capacity, column(probs, EXPERT_AT + expert), 0.0)
            prob_ref[here, :] = jnp.where(lane == SHARE_AT, share, probs)
            kept = jnp.where(slot < capacity, 1.0, 0.0)
            scale_ref[here, :] = jnp.where(
                lane == 0, gate, jnp.where(lane == 1, share, jnp.where(lane == 2, kept, 0.0))
            )
        dot_ref[...] = jnp.zeros_like(dot_ref)

    for at in range(0, tokens, step):
        here = pl.ds(at, step)
        gate_up = mm(h_ref[here, :], up_ref[...])
        back = mm(dy_ref[here, :width], down_ref[...])
        gate, up = gate_up[:, :UNITS], gate_up[:, UNITS:]
        scale = jnp.where(routed, scale_ref[here, 0:1], scale_ref[here, 1:2])
        counts = jnp.where(routed, scale_ref[here, 2:3], 1.0)
        sigma = jax.nn.sigmoid(gate)
        silu = gate * sigma
        act = (silu * up).astype(BF).astype(F32)
        dots = jnp.sum(act * back, axis=1, keepdims=True) * counts
        dot_ref[here, :] += jnp.where(lane == jnp.where(routed, expert, EXPERTS), dots, 0.0)
        back = back * scale
        act_ref[here, :] = (act * scale).astype(BF)
        middle_ref[here, :UNITS] = (back * up * sigma * (1.0 + gate * (1.0 - sigma))).astype(BF)
        middle_ref[here, UNITS:] = (back * silu).astype(BF)


def feed_forward(h, others, weights, misc, expert, capacity):
    tokens, width = h.shape
    parts = weights.shape[1] // (3 * UNITS)

    def whole(shape):
        return pl.BlockSpec(shape, lambda i, e: (0, 0), pipeline_mode=pl.Buffered(1))

    return pl.pallas_call(
        functools.partial(feed_forward_kernel, capacity),
        grid_spec=pltpu.PrefetchScalarGridSpec(
            num_scalar_prefetch=1,
            grid=(parts,),
            in_specs=[
                whole(h.shape),
                whole((tokens, width + LANES)),
                pl.BlockSpec((width, 2 * UNITS), lambda i, e: (0, i)),
                pl.BlockSpec((width, UNITS), lambda i, e: (0, 2 * parts + i)),
                whole(misc.shape),
            ],
            out_specs=[
                pl.BlockSpec((tokens, 2 * UNITS), lambda i, e: (0, i)),
                pl.BlockSpec((tokens, UNITS), lambda i, e: (0, i)),
                pl.BlockSpec((tokens, LANES), lambda i, e: (0, 0)),
                pl.BlockSpec((tokens, LANES), lambda i, e: (0, 0)),
            ],
            scratch_shapes=[pltpu.VMEM((tokens, LANES), F32)],
        ),
        out_shape=[
            jax.ShapeDtypeStruct((tokens, 2 * UNITS * parts), BF),
            jax.ShapeDtypeStruct((tokens, UNITS * parts), BF),
            jax.ShapeDtypeStruct((tokens, LANES), F32),
            jax.ShapeDtypeStruct((tokens, LANES), F32),
        ],
        compiler_params=pltpu.CompilerParams(vmem_limit_bytes=VMEM),
    )(expert, h, others, weights, weights, misc)


def ffn_rest_kernel(h_ref, dy_ref, middle_ref, act_ref, down_ref, grad_ref, out_ref):
    ups = middle_ref.shape[1]
    grad_ref[:, :ups] = mm_tn(h_ref[...], middle_ref[...]).astype(BF)
    grad_ref[:, ups:] = mm_tn(dy_ref[...], act_ref[...]).astype(BF)
    out_ref[...] = mm_nt(act_ref[...], down_ref[...]).astype(BF)


def ffn_rest(h, dy, middle, act, weights):
    tokens, width = h.shape
    ups, downs = middle.shape[1], act.shape[1]
    step = 256
    return pl.pallas_call(
        ffn_rest_kernel,
        grid=(width // step,),
        in_specs=[
            pl.BlockSpec((tokens, step), lambda i: (0, i)),
            pl.BlockSpec((tokens, step), lambda i: (0, i)),
            pl.BlockSpec((tokens, ups), lambda i: (0, 0)),
            pl.BlockSpec((tokens, downs), lambda i: (0, 0)),
            pl.BlockSpec((step, downs), lambda i: (i, ups // downs)),
        ],
        out_specs=[
            pl.BlockSpec((step, ups + downs), lambda i: (i, 0)),
            pl.BlockSpec((tokens, step), lambda i: (0, i)),
        ],
        out_shape=[
            jax.ShapeDtypeStruct((width, ups + downs), BF),
            jax.ShapeDtypeStruct((tokens, width), BF),
        ],
        compiler_params=pltpu.CompilerParams(vmem_limit_bytes=VMEM),
    )(h, dy, middle, act, weights)


def attn_grads_kernel(h_ref, linear_ref, small_ref, dx_ref, heads_ref, grad_ref):
    qkv = linear_ref.shape[1]
    grad_ref[:, :qkv] = mm_tn(h_ref[...], linear_ref[...]).astype(BF)
    grad_ref[:, qkv : qkv + LANES] = small_ref[...].T.astype(BF)
    grad_ref[:, qkv + LANES :] = mm_tn(dx_ref[...], heads_ref[...]).astype(BF)


def attn_grads(h, linear, small, dx, heads):
    tokens, width = h.shape
    rows, heads_width = heads.shape
    qkv = linear.shape[1]
    columns = qkv + LANES + heads_width
    step = 256
    return pl.pallas_call(
        attn_grads_kernel,
        grid=(width // step,),
        in_specs=[
            pl.BlockSpec((tokens, step), lambda i: (0, i)),
            pl.BlockSpec((tokens, qkv), lambda i: (0, 0)),
            pl.BlockSpec((LANES, step), lambda i: (0, i)),
            pl.BlockSpec((rows, step), lambda i: (0, i)),
            pl.BlockSpec((rows, heads_width), lambda i: (0, 0)),
        ],
        out_specs=pl.BlockSpec((step, columns), lambda i: (i, 0)),
        out_shape=jax.ShapeDtypeStruct((width, columns), BF),
        compiler_params=pltpu.CompilerParams(vmem_limit_bytes=VMEM),
    )(h, linear, small, dx, heads)


def plane_gather(x):
    n, width = x.shape
    count = lax.axis_size(SEQ) * lax.axis_size("tensor")
    copies = jnp.broadcast_to(x[None], (count, n, width))
    return lax.all_to_all(copies, GRID, 0, 0, tiled=True).reshape(count * n, width)


def send_parts(parts):
    count = lax.axis_size(SEQ) * lax.axis_size("tensor")
    parts = parts.astype(BF).reshape(count, -1, parts.shape[-1])
    return lax.all_to_all(parts, GRID, 0, 0, tiled=True)


def sum_parts(parts):
    return jnp.sum(parts.astype(F32), axis=0)


def plane_scatter(parts):
    return sum_parts(send_parts(parts))


def body(
    hidden_in,
    grad_out,
    expert_ids,
    slot_rank,
    piece_start,
    norm_attn,
    w_qkv,
    b_qkv,
    w_proj,
    norm_ffn,
    w_router,
    w_share_gate,
    expert_gate_up,
    expert_down,
    shared_gate_up,
    shared_down,
):
    seqs = lax.axis_size(SEQ)
    dps = lax.axis_size("dp")
    me_seq = lax.axis_index(SEQ)
    me_tensor = lax.axis_index("tensor")
    me = me_seq * 2 + me_tensor
    rows = hidden_in.shape[1]
    own = rows // 2
    length = rows * seqs
    depth = w_qkv.shape[0]
    width = depth * dps * seqs
    experts = expert_gate_up.shape[1]
    fe = expert_gate_up.shape[3]
    fs = shared_gate_up.shape[2] // seqs
    fe_pad = up_to(fe, UNITS)
    fs_pad = up_to(fs, UNITS)
    bias_part = b_qkv.shape[2]
    heads = b_qkv.shape[1]
    capacity = (5 * rows * TOPK + 4 * experts - 1) // (4 * experts)
    score_scale = 1.0 / math.sqrt(HD)

    def mine(x):
        return lax.dynamic_slice_in_dim(x, me_tensor * own, own, 0)

    def both_halves(x):
        other = swap(x)
        first = jnp.where(me_tensor == 0, x, other)
        second = jnp.where(me_tensor == 0, other, x)
        return jnp.concatenate([first, second], 0)

    flat_ids = expert_ids[0].reshape(-1)
    flat_rank = slot_rank[0].reshape(-1)
    earlier = (flat_rank[None, :] < flat_rank[:, None]) & (flat_ids[None, :] == flat_ids[:, None])
    position = jnp.sum(earlier.astype(jnp.int32), axis=1)
    position = jnp.where(position < capacity, position, LANES - 1)
    chosen = expert_ids[0][:, :, None] == jnp.arange(experts, dtype=jnp.int32)[None, None, :]
    slot_of = jnp.sum(
        jnp.where(chosen, position.reshape(rows, TOPK)[:, :, None] - (LANES - 1), 0), axis=1
    ) + (LANES - 1)
    slot_cols = jnp.pad(slot_of.astype(BF), ((0, 0), (0, LANES - experts)))
    dy_own = mine(grad_out[0])
    x_own = mine(hidden_in[0])

    misc = jnp.concatenate(
        [norm_attn[:, None], norm_ffn[:, None], w_share_gate[:, None], w_router], axis=1
    )
    n_misc = misc.shape[1]
    bias_rows = b_qkv.transpose(1, 0, 2).reshape(heads, 3 * bias_part)
    bias_rows = jnp.pad(bias_rows, ((0, 0), (0, depth - 3 * bias_part)))
    attn_blob = jnp.concatenate(
        [
            w_qkv.reshape(depth, 3, heads, HD).transpose(2, 0, 1, 3).reshape(heads, depth, 3 * HD),
            jnp.broadcast_to(misc[None], (heads, depth, n_misc)),
            bias_rows[:, :, None],
            jnp.zeros((heads, depth, LANES - n_misc - 1), BF),
            jnp.broadcast_to(w_proj.T[None], (heads, depth, heads * HD)),
        ],
        axis=2,
    )
    def padded(x, units):
        return jnp.pad(x, ((0, 0), (0, 0), (0, units - x.shape[2])))

    units = fe_pad + fs_pad
    egu_blob = expert_gate_up.transpose(1, 2, 0, 3)
    sgu_blob = shared_gate_up.reshape(depth, 2, seqs, fs).transpose(2, 1, 0, 3)
    edn_blob = expert_down.transpose(0, 2, 1)
    sdn_blob = shared_down.reshape(seqs, fs, depth).transpose(0, 2, 1)
    columns = []
    for blob, blob_units in ((egu_blob, fe_pad), (sgu_blob, fs_pad)):
        gates, ups = padded(blob[:, 0], blob_units), padded(blob[:, 1], blob_units)
        for at in range(0, blob_units, UNITS):
            columns += [gates[:, :, at : at + UNITS], ups[:, :, at : at + UNITS]]
    columns += [padded(edn_blob, fe_pad), padded(sdn_blob, fs_pad)]
    ffn_blob = jnp.concatenate(columns, axis=2)

    first_ring = lax.axis_index("z_hi") == 0

    def both_rings(block):
        facing = from_facing(block)
        return jnp.stack(
            [jnp.where(first_ring, block, facing), jnp.where(first_ring, facing, block)]
        )

    x_all = lax.all_gather(both_rings(hidden_in[0]), "ring", axis=1, tiled=True)
    x_all = x_all.reshape(length, width)
    dy_slots = both_rings(jnp.concatenate([grad_out[0], slot_cols], 1))

    attn_blob = lax.all_to_all(attn_blob, SEQ, 0, 0, tiled=True).reshape(seqs * depth, -1)
    attn_cols = 3 * HD + LANES
    proj_rows = attn_blob[:, attn_cols:]
    attn_full = jnp.broadcast_to(attn_blob[None, :, :attn_cols], (dps, seqs * depth, attn_cols))
    attn_full = lax.all_to_all(attn_full, "dp", 0, 0, tiled=True).reshape(width, -1)
    x_all, attn_full, proj_rows, ffn_blob, dy_slots = together(
        x_all, attn_full, proj_rows, ffn_blob, dy_slots
    )
    proj_rows = lax.all_gather(proj_rows, "dp", axis=0, tiled=True)
    qkv_full = attn_full[:, : 3 * HD]
    misc_full = attn_full[:, 3 * HD :]
    ffn_blob = lax.all_to_all(ffn_blob, SEQ, 0, 0, tiled=True)

    bias_full = misc_full[:, n_misc].reshape(dps * seqs, depth)[:, : 3 * bias_part]
    bias_full = bias_full.reshape(dps * seqs, 3, bias_part).transpose(1, 0, 2).reshape(1, 3 * HD)
    misc_rows = misc_full[:, :n_misc].T.astype(F32)
    gain_attn = misc_rows[0:1]
    gain_ffn = misc_rows[1:2]

    positions = jnp.arange(length, dtype=jnp.int32)
    freq_table = jnp.exp(jnp.arange(HD // 2, dtype=F32) * (-2.0 * math.log(THETA) / HD))
    angle = positions.astype(F32)[:, None] * freq_table[None, :]
    cosine = jnp.cos(angle)
    sine = jnp.sin(angle)
    starts = piece_start[0]
    inside = (positions[:, None] >= starts[None, :]) & (
        positions[:, None] < starts[None, :] + PIC
    )
    labels = jnp.arange(starts.shape[0], dtype=jnp.int32)
    segment = jnp.max(jnp.where(inside, labels[None, :], -1), axis=1)

    def seen():
        causal = positions[None, :] <= positions[:, None]
        picture = (segment[:, None] == segment[None, :]) & (segment[:, None] >= 0)
        return causal | picture

    def rotate(values):
        lead, tail = values[:, : HD // 2], values[:, HD // 2 :]
        return jnp.concatenate([lead * cosine - tail * sine, tail * cosine + lead * sine], axis=1)

    def unrotate(values):
        lead, tail = values[:, : HD // 2], values[:, HD // 2 :]
        return jnp.concatenate([lead * cosine + tail * sine, tail * cosine - lead * sine], axis=1)

    resid_all = x_all.astype(F32)
    norm_one = resid_all * rms_scale(resid_all)
    normed_one = (norm_one * gain_attn).astype(BF)
    linear = mm(normed_one, qkv_full) + bias_full.astype(F32)
    query = rotate(linear[:, :HD]).astype(BF)
    key = rotate(linear[:, HD : 2 * HD]).astype(BF)
    value = linear[:, 2 * HD :].astype(BF)
    scores = jnp.where(seen(), mm_nt(query, key) * score_scale, MASKED)
    exp_scores = jnp.exp(scores - jnp.max(scores, axis=1, keepdims=True))
    attn_probs = exp_scores / jnp.sum(exp_scores, axis=1, keepdims=True)
    probs_low = attn_probs.astype(BF)
    attn_head = mm(probs_low, value).astype(BF)

    by_head, ffn_blob, dy_slots, proj_rows = together(
        attn_head.reshape(seqs, rows, HD), ffn_blob, dy_slots, proj_rows
    )
    by_head = lax.all_to_all(by_head, SEQ, 0, 0, tiled=True)
    dy_slots = lax.all_gather(dy_slots, "ring", axis=1, tiled=True)
    attn_flat = by_head.transpose(1, 0, 2).reshape(rows, heads * HD)
    attn_part = mm_nt(attn_flat, proj_rows)
    theirs = lax.dynamic_slice_in_dim(attn_part, (1 - me_tensor) * own, own, 0)
    attn_sum = mine(attn_part) + swap(theirs.astype(BF)).astype(F32)
    after_attn = x_own.astype(F32) + attn_sum
    scale_two = rms_scale(after_attn)
    norm_two = after_attn * scale_two
    normed_two = (norm_two * gain_ffn).astype(BF)
    ffn_blob, dy_slots, normed_sent = together(
        ffn_blob, dy_slots.reshape(length, width + LANES), normed_two
    )
    h_all = plane_gather(normed_sent)
    ffn_full = lax.all_gather(ffn_blob.reshape(seqs * depth, -1), "dp", axis=0, tiled=True)
    w_up = ffn_full[:, : 2 * units]

    expert = me_seq.astype(jnp.int32).reshape(1)
    dgate_up, act_weighed, dots, router = feed_forward(
        h_all, dy_slots, ffn_full, misc_full, expert, capacity
    )
    back_parts = jnp.concatenate([mm_nt(dgate_up, w_up).astype(BF), dots.astype(BF)], 1)
    half = width // 2
    ffn_left = send_parts(mm_nt(act_weighed, ffn_full[:half, 2 * units :]))
    back_parts, act_weighed, dgate_up, ffn_left = together(
        back_parts, act_weighed, dgate_up, ffn_left
    )
    back = send_parts(back_parts)

    ffn_grad, ffn_parts = ffn_rest(h_all, dy_slots, dgate_up, act_weighed, ffn_full)
    back, ffn_parts, ffn_grad = together(back, ffn_parts, ffn_grad)
    back = sum_parts(back)
    ffn_grad = lax.psum_scatter(ffn_grad, "dp", scatter_dimension=0, tiled=True)

    router_own = lax.dynamic_slice_in_dim(router, me * own, own, 0)
    probs_own = router_own[:, EXPERT_AT : EXPERT_AT + experts]
    sig_own = router_own[:, SHARE_AT : SHARE_AT + 1]
    dprobs = back[:, width : width + experts]
    dlogits = probs_own * (dprobs - jnp.sum(probs_own * dprobs, axis=1, keepdims=True))
    dshare = back[:, width + experts : width + experts + 1] * sig_own * (1.0 - sig_own)
    dmisc = jnp.concatenate([jnp.zeros((own, 2), F32), dshare, dlogits], 1)
    dmisc = jnp.pad(dmisc, ((0, 0), (0, LANES - n_misc))).astype(BF)
    dh_two = back[:, :width] + mm_nt(dmisc, misc_full)
    grad_misc = mm_tn(dmisc, normed_two)
    grad_gain_ffn = jnp.sum(dh_two * norm_two, axis=0)
    inner_two = dh_two * gain_ffn
    dx_one = dy_own.astype(F32) + scale_two * (
        inner_two - norm_two * jnp.mean(inner_two * norm_two, axis=-1, keepdims=True)
    )
    dx_low = dx_one.astype(BF)

    dx_pair = both_halves(dx_low)
    do_flat = mm(dx_pair, proj_rows).astype(BF)
    do_heads = do_flat.reshape(rows, heads, HD).transpose(1, 0, 2)
    do_head = lax.all_to_all(do_heads, SEQ, 0, 0, tiled=True).reshape(length, HD)
    do_head, ffn_right = together(do_head, ffn_parts[:, half:])
    ffn_right = send_parts(ffn_right)
    dvalue = mm_tn(probs_low, do_head)
    dprob = mm_nt(do_head, value)
    row_delta = jnp.sum(attn_probs * dprob, axis=1, keepdims=True)
    dscore = (attn_probs * (dprob - row_delta)).astype(BF)
    dquery = mm(dscore, key) * score_scale
    dkey = mm_tn(dscore, query) * score_scale
    dlinear = jnp.concatenate([unrotate(dquery), unrotate(dkey), dvalue], 1).astype(BF)
    grad_bias = jnp.sum(dlinear.astype(F32), axis=0)
    dh_part = mm_nt(dlinear, qkv_full)
    grad_gain_attn = jnp.sum(dh_part * norm_one, axis=0)
    dh_low, ffn_right = together(dh_part.astype(BF), ffn_right)
    dh_sent = send_parts(dh_low)
    ffn_sum = jnp.concatenate([sum_parts(ffn_left), sum_parts(ffn_right)], 1)
    hidden_out = both_halves((after_attn + ffn_sum).astype(BF))

    bias_rows = grad_bias.reshape(3, dps * seqs, bias_part).transpose(1, 0, 2)
    bias_rows = bias_rows.reshape(dps * seqs, 3 * bias_part)
    bias_rows = jnp.pad(bias_rows, ((0, 0), (0, depth - 3 * bias_part))).reshape(1, width)
    small = jnp.concatenate(
        [grad_gain_attn[None], grad_gain_ffn[None], grad_misc[2:n_misc], bias_rows], 0
    )
    small = jnp.pad(small, ((0, LANES - n_misc - 1), (0, 0)))
    attn_grad = attn_grads(normed_one, dlinear, small, dx_pair, attn_flat)
    dh_sent, attn_grad, ffn_grad, hidden_out = together(
        dh_sent, attn_grad, ffn_grad, hidden_out
    )
    attn_grad = lax.psum_scatter(attn_grad, "dp", scatter_dimension=0, tiled=True)
    dh_one = sum_parts(dh_sent)
    resid = x_own.astype(F32)
    scale_one = rms_scale(resid)
    norm_own = resid * scale_one
    inner_one = dh_one * gain_attn
    grad_in = dx_one + scale_one * (
        inner_one - norm_own * jnp.mean(inner_one * norm_own, axis=-1, keepdims=True)
    )
    grad_in = both_halves(grad_in)
    ffn_grad = lax.all_to_all(ffn_grad.reshape(seqs, depth, -1), SEQ, 0, 0, tiled=True)
    ffn_grad, attn_grad, grad_in = together(ffn_grad, attn_grad, grad_in)
    attn_grad = attn_grad.reshape(seqs, depth, -1)
    attn_grad = lax.all_to_all(attn_grad, SEQ, 0, 0, tiled=True).astype(F32)

    def unit_columns(first, kind, size):
        at = [(2 * (first + i) + kind) * UNITS for i in range(up_to(size, UNITS) // UNITS)]
        picked = [
            ffn_grad[:, :, c : c + min(UNITS, size - i * UNITS)] for i, c in enumerate(at)
        ]
        return jnp.concatenate(picked, 2).astype(F32)

    shared_at = fe_pad // UNITS
    out_egu = jnp.stack([unit_columns(0, 0, fe), unit_columns(0, 1, fe)], 2).transpose(1, 0, 2, 3)
    out_sgu = [unit_columns(shared_at, kind, fs).transpose(1, 0, 2) for kind in (0, 1)]
    out_sgu = jnp.stack(out_sgu, 1).reshape(depth, 2, seqs * fs)
    down_at = 2 * units
    out_edn = ffn_grad[:, :, down_at : down_at + fe].transpose(0, 2, 1).astype(F32)
    out_sdn = ffn_grad[:, :, down_at + fe_pad : down_at + fe_pad + fs].transpose(0, 2, 1)
    out_sdn = out_sdn.reshape(seqs * fs, depth).astype(F32)
    out_qkv = attn_grad[:, :, : 3 * HD].reshape(heads, depth, 3, HD)
    out_qkv = out_qkv.transpose(1, 2, 0, 3).reshape(depth, 3, heads * HD)
    out_misc = jnp.sum(attn_grad[:, :, 3 * HD : 3 * HD + n_misc], axis=0)
    out_misc = out_misc + swap(out_misc)
    out_bias = attn_grad[:, : 3 * bias_part, 3 * HD + n_misc]
    out_bias = out_bias.reshape(heads, 3, bias_part).transpose(1, 0, 2)
    out_proj = jnp.sum(attn_grad[:, :, 3 * HD + LANES :], axis=0).T

    return (
        hidden_out[None],
        grad_in[None],
        out_misc[:, 0],
        out_qkv,
        out_bias,
        out_proj,
        out_misc[:, 1],
        out_misc[:, 3:n_misc],
        out_misc[:, 2],
        out_egu,
        out_edn,
        out_sgu,
        out_sdn,
    )


def solution(mesh):
    in_specs = (
        P("dp", SEQ, None),
        P("dp", SEQ, None),
        P("dp", SEQ, None),
        P("dp", SEQ, None),
        P("dp", None),
        P(("dp", *SEQ)),
        P(("dp", *SEQ), None, "tensor"),
        P(None, "tensor", ("dp", *SEQ)),
        P("tensor", ("dp", *SEQ)),
        P(("dp", *SEQ)),
        P(("dp", *SEQ), None),
        P(("dp", *SEQ)),
        P(("dp", *SEQ), None, None, "tensor"),
        P(None, "tensor", ("dp", *SEQ)),
        P(("dp", *SEQ), None, "tensor"),
        P("tensor", ("dp", *SEQ)),
    )
    out_specs = (
        P("dp", SEQ, None),
        P("dp", SEQ, None),
        P(("dp", *SEQ)),
        P(("dp", *SEQ), None, "tensor"),
        P(None, "tensor", ("dp", *SEQ)),
        P("tensor", ("dp", *SEQ)),
        P(("dp", *SEQ)),
        P(("dp", *SEQ), None),
        P(("dp", *SEQ)),
        P(("dp", *SEQ), None, None, "tensor"),
        P(None, "tensor", ("dp", *SEQ)),
        P(("dp", *SEQ), None, "tensor"),
        P("tensor", ("dp", *SEQ)),
    )
    fine = Mesh(mesh.devices.reshape(mesh.shape["dp"], 2, -1, 2), ("dp", *SEQ, "tensor"))
    return jax.shard_map(body, mesh=fine, in_specs=in_specs, out_specs=out_specs, check_vma=False)
```
